512 devices in a mesh: plane: 64 (over z, y), dom: 8 (over x, core).
Axes of the slice: x: 4, y: 8, z: 8, core: 2. Of those that a mesh axis runs over, the one named last changes fastest.
Arguments:
- spectral_fields: float32 [4, 256, 512, 128], P(None, 'plane', 'dom')
- deriv_ops: float32 [2, 128, 128], replicated, may hold values from -0.5 to 0.5
- geom: float32 [2, 512, 128], P(None, 'dom'), may hold values from 0.5 to 2
- stiffness: float32 [128, 128], replicated, as said below
- stiff_scale: float32 [512], P('dom'), may hold values from 0.3 to 3
- traces: float32 [4, 16, 128], replicated, may hold values from -0.5 to 0.5
- neighbors: int32 [512, 4], P('dom'), may hold values from -2 to 511, as said below
- rim_lists: int32 [8, 2, 32], P('dom'), may hold values from 0 to 63, as said below
- melt_flags: int32 [256, 512], P(None, ('dom', 'plane')), may hold values 0 or 1
Outputs:
- momentum_terms: float32 [3, 256, 512, 128], P(None, 'plane', 'dom')
- temperature_next: float32 [256, 512, 128], P('plane', 'dom')
The draws below stay inside these ranges and needn't reach their ends.
Inputs may be any that keep to these rules, and one draw needn't show every extreme that they name: stiffness is symmetric. `neighbors`: elements 64 d to 64 (d + 1) - 1 form partition d, 2 columns around the tube by 32 elements radially. Edges 0 and 2 are radial, -1 at the tube's walls; edges 1 and 3 go around the tube, -2 where the element across lies in the next or previous partition (cyclically), which happens for exactly 32 elements of each partition on each side. Two elements that face each other name each other across edges j and (j + 2) mod 4. Local numbers (0 to 63 within the partition): rim_lists[d, 0] lists the elements of partition d marked -2 across edge 3, rim_lists[d, 1] those marked -2 across edge 1, each once.
All inputs are finite; a program needn't handle non-finite values. No bound on the sum of `melt_flags` on one device may be relied on, other than what follows from the above.
Results may differ from the reference program's by a relative error of at most 0.00011.
Values sent between devices are 32-bit elements; how exact they have to be, the bound alone decides.
No kernel may reach another device: no remote copies, remote signals or barrier semaphores. Data moves between devices by JAX's collectives and lax.ppermute only.
A program may use at most 64 MiB of HBM per device.

```python
import math
import jax
import jax.numpy as jnp
from jax import lax

PLANES = 256
POINTS = 128
TRACE = 16
RAD = 32
TH_DEV = 2
ITERS = 2
ELEM_DEV = 64
DOMS = 8
ELEMENTS = 512


def draw_spectral_fields(key, part):
    base_key = jax.random.fold_in(key, 3)
    field_key, scale_key = jax.random.split(base_key, 2)
    full_shape = (4, PLANES, ELEMENTS, POINTS)
    samples = jax.random.normal(field_key, full_shape, jnp.float32)
    element_ids = jnp.arange(ELEMENTS).astype(jnp.float32)
    rising = 0.6 + 1.2 * element_ids / ELEMENTS
    spread = 10.0 ** jax.random.uniform(scale_key, (ELEMENTS,), jnp.float32, -0.5, 0.5)
    scales = jnp.concatenate([0.7 * jnp.ones((3, ELEMENTS), jnp.float32), (rising * spread)[None]], axis=0)
    return samples * scales[:, None, :, None]


def draw_stiffness(key, part):
    base_key = jax.random.fold_in(key, 5)
    off_key, diag_key = jax.random.split(base_key, 2)
    raw = jax.random.uniform(off_key, (POINTS, POINTS), jnp.float32, -1.0, 1.0) / POINTS
    symmetric = 0.5 * (raw + jnp.transpose(raw))
    diagonal = 1.0 + jax.random.uniform(diag_key, (POINTS,), jnp.float32, 0.0, 0.5)
    identity_mask = jnp.arange(POINTS)[:, None] == jnp.arange(POINTS)[None, :]
    return jnp.where(identity_mask, diagonal[None, :], symmetric)


def element_layout(key):
    layout_key = jax.random.fold_in(key, 11)
    part_keys = jax.random.split(layout_key, DOMS)

    def permute(one_key):
        return jax.random.permutation(one_key, ELEM_DEV)
    orders = jax.vmap(permute)(part_keys).astype(jnp.int32)
    cell_of = jnp.argsort(orders, axis=1).astype(jnp.int32)
    return (orders, cell_of)


def draw_neighbors(key, part):
    orders, cell_of = element_layout(key)
    dom_ids = jnp.arange(DOMS)[:, None]
    beside_all = cell_of // RAD
    radial = cell_of % RAD

    def global_id(partition, around_pos, radial_pos):
        return partition * ELEM_DEV + orders[partition, around_pos * RAD + radial_pos]
    outward = jnp.where(radial + 1 < RAD, global_id(dom_ids, beside_all, jnp.minimum(radial + 1, RAD - 1)), -1)
    inward = jnp.where(radial >= 1, global_id(dom_ids, beside_all, jnp.maximum(radial - 1, 0)), -1)
    forward = jnp.where(beside_all + 1 < TH_DEV, global_id(dom_ids, jnp.minimum(beside_all + 1, TH_DEV - 1), radial), -2)
    backward = jnp.where(beside_all >= 1, global_id(dom_ids, jnp.maximum(beside_all - 1, 0), radial), -2)
    neighbor_table = jnp.stack([outward, forward, inward, backward], axis=-1)
    return neighbor_table.reshape(ELEMENTS, 4).astype(jnp.int32)


def draw_rim_lists(key, part):
    orders, cell_of = element_layout(key)
    left_side = orders[:, 0:RAD]
    right_side = orders[:, (TH_DEV - 1) * RAD:TH_DEV * RAD]
    return jnp.stack([left_side, right_side], axis=1).astype(jnp.int32)


def plant(result, rng, least, largest):
    shape = result.shape
    spot = [jax.random.randint(jax.random.fold_in(rng, axis), (), 0, shape[axis]) for axis in range(len(shape))]
    result = result.at[tuple(spot)].set(least)
    longest = shape.index(max(shape))
    spot[longest] = (spot[longest] + 1) % shape[longest]
    return result.at[tuple(spot)].set(largest)


def level_of(own_key, dims, cuts, least, largest):
    level, own = 1.0, jax.random.fold_in(own_key, 6)
    for position, parts in cuts:
        draws = jnp.exp(jax.random.uniform(jax.random.fold_in(own, position), (parts,), jnp.float32, least / len(cuts), largest / len(cuts)))
        level = level * jnp.repeat(draws, dims[position] // parts).reshape([-1 if axis == position else 1 for axis in range(len(dims))])
    return level


def normal_values(key, extent, width, limit, kind=jnp.bfloat16):
    drawn = jax.random.normal(key, extent, jnp.float32) * width
    return jnp.minimum(jnp.maximum(drawn, -limit), limit).astype(kind)


def setup_inputs(seed: int = 0) -> dict:
    keys = jax.random.split(jax.random.key(seed), 10)
    return {
        "spectral_fields": draw_spectral_fields(jax.random.fold_in(keys[9], 71), 0),
        "deriv_ops": normal_values(keys[1], (2, POINTS, POINTS), POINTS ** -0.5, 0.5, jnp.float32),
        "geom": jnp.clip(jnp.exp(math.log(2.0) - 1.3862944 * jax.random.uniform(keys[2], (2, ELEMENTS, POINTS), jnp.float32) ** level_of(keys[2], (2, ELEMENTS, POINTS), ((1, 8),), -0.2, 0.2)), 0.5, 2.0),
        "stiffness": draw_stiffness(jax.random.fold_in(keys[9], 71), 0),
        "stiff_scale": jnp.clip(jnp.exp(math.log(3.0) - 2.3025851 * jax.random.uniform(keys[4], (ELEMENTS,), jnp.float32) ** level_of(keys[4], (ELEMENTS,), ((0, 8),), -0.2, 0.2)), 0.3, 3.0),
        "traces": normal_values(keys[5], (4, TRACE, POINTS), POINTS ** -0.5, 0.5, jnp.float32),
        "neighbors": draw_neighbors(jax.random.fold_in(keys[9], 71), 0),
        "rim_lists": draw_rim_lists(jax.random.fold_in(keys[9], 71), 0),
        "melt_flags": plant((jax.random.randint(keys[8], (PLANES, ELEMENTS), 0, 3) < 1).astype(jnp.int32), jax.random.fold_in(keys[8], 1), 0, 1),
    }


inverse_step = 0.5
penalty_weight = 1.0
latent_heat = 2.0
axial_wave = 0.01


def axial_tables(planes):
    point_ids = jnp.arange(planes)[:, None]
    plane_ids = jnp.arange(planes)[None, :]
    mode_number = jnp.where(plane_ids == 1, planes // 2, plane_ids // 2)
    phase_index = (point_ids * mode_number) % planes
    angles = (2.0 * jnp.pi / planes) * phase_index.astype(jnp.float32)
    sine_plane = (plane_ids % 2 == 1) & (plane_ids != 1)
    axial_basis = jnp.where(sine_plane, jnp.sin(angles), jnp.cos(angles))
    wave_number = jnp.where(plane_ids >= 2, mode_number, 0).astype(jnp.float32) * axial_wave
    axial_slope = wave_number * jnp.where(sine_plane, jnp.cos(angles), -jnp.sin(angles))
    weights = jnp.where(plane_ids <= 1, 1.0 / planes, 2.0 / planes)
    modal_basis = jnp.transpose(weights * axial_basis)
    return axial_basis, axial_slope, modal_basis


def squared_waves(plane_ids, planes):
    mode_number = jnp.where(plane_ids == 1, planes // 2, plane_ids // 2)
    return (mode_number.astype(jnp.float32) * axial_wave) ** 2


def reference(spectral_fields, deriv_ops, geom, stiffness, stiff_scale, traces, neighbors, rim_lists, melt_flags):
    highest = lax.Precision.HIGHEST
    axial_basis, axial_slope, modal_basis = axial_tables(PLANES)

    def block_terms(start):
        fields = lax.dynamic_slice_in_dim(spectral_fields, start, RAD, 2)
        factors = lax.dynamic_slice_in_dim(geom, start, RAD, 1)
        flags = lax.dynamic_slice_in_dim(melt_flags, start, RAD, 1)
        values = jnp.einsum("mp,cpen->cmen", axial_basis, fields, precision=highest)
        axial_values = jnp.einsum("mp,cpen->cmen", axial_slope, fields, precision=highest)
        first_slope = factors[0][None, None] * jnp.einsum("cmen,kn->cmek", values, deriv_ops[0], precision=highest)
        second_slope = factors[1][None, None] * jnp.einsum("cmen,kn->cmek", values, deriv_ops[1], precision=highest)
        advection = -(values[0][None] * first_slope + values[1][None] * second_slope + values[2][None] * axial_values)
        heat_terms = advection[3] / (1.0 + latent_heat * flags.astype(jnp.float32))[:, :, None]
        all_terms = jnp.concatenate([advection[:3], heat_terms[None]], axis=0)
        return jnp.einsum("pm,cmen->cpen", modal_basis, all_terms, precision=highest)

    starts = (jnp.arange(ELEMENTS // RAD) * RAD).astype(jnp.int32)
    blocks = lax.map(block_terms, starts)
    modal_terms = jnp.transpose(blocks, (1, 2, 0, 3, 4)).reshape(4, PLANES, ELEMENTS, POINTS)

    part_ids = jnp.arange(DOMS)
    following = (part_ids + 1) % DOMS
    preceding = (part_ids - 1) % DOMS
    right_global = (part_ids[:, None] * ELEM_DEV + rim_lists[:, 1, :]).reshape(-1)
    left_next = (following[:, None] * ELEM_DEV + rim_lists[following, 0, :]).reshape(-1)
    left_global = (part_ids[:, None] * ELEM_DEV + rim_lists[:, 0, :]).reshape(-1)
    right_prev = (preceding[:, None] * ELEM_DEV + rim_lists[preceding, 1, :]).reshape(-1)
    forward = neighbors[:, 1].at[right_global].set(left_next.astype(jnp.int32))
    backward = neighbors[:, 3].at[left_global].set(right_prev.astype(jnp.int32))
    across = jnp.stack([neighbors[:, 0], forward, neighbors[:, 2], backward], axis=1)

    wave_squares = squared_waves(jnp.arange(PLANES), PLANES)[:, None, None]

    def helmholtz(vector):
        edge_values = jnp.einsum("jtn,pen->jtpe", traces, vector, precision=highest)
        facing = []
        for edge_number in range(4):
            column = across[:, edge_number]
            source = edge_values[(edge_number + 2) % 4]
            picked = jnp.take(source, jnp.clip(column, 0, ELEMENTS - 1), axis=2)
            facing.append(picked * (column >= 0).astype(jnp.float32)[None, None, :])
        trace_jumps = edge_values - jnp.stack(facing, axis=0)
        coupling = jnp.einsum("jtn,jtpe->pen", traces, trace_jumps, precision=highest)
        stiff_part = jnp.dot(vector.reshape(-1, POINTS), stiffness, precision=highest).reshape(vector.shape)
        return (inverse_step + wave_squares) * vector + stiff_scale[None, :, None] * stiff_part + penalty_weight * coupling

    def plane_sums(first_field, second_field):
        return jnp.sum(first_field * second_field, axis=(1, 2))

    right_hand = inverse_step * spectral_fields[3] + modal_terms[3]
    solution = spectral_fields[3]
    residual = right_hand - helmholtz(solution)
    search = residual
    norm_now = plane_sums(residual, residual)
    for iteration in range(ITERS):
        applied = helmholtz(search)
        step_size = norm_now / plane_sums(search, applied)
        solution = solution + step_size[:, None, None] * search
        residual = residual - step_size[:, None, None] * applied
        norm_next = plane_sums(residual, residual)
        search = residual + (norm_next / norm_now)[:, None, None] * search
        norm_now = norm_next
    return modal_terms[:3], solution
```

```python
import functools

import jax
import jax.numpy as jnp
import numpy as np
from jax import lax
from jax.experimental import pallas as pl
from jax.experimental.pallas import tpu as pltpu
from jax.sharding import PartitionSpec as P

PLANES = 256
POINTS = 128
ELEMS = 64
OWN = 4
EDGES = 4
TRACE = 16
RIM = 32
ROWS = OWN * ELEMS
AXIAL_WAVE = 0.01
INVERSE_STEP = 0.5
LATENT = 2.0
F32 = jnp.float32
BF16 = jnp.bfloat16


def halves_np(table):
    high = table.astype(np.float32).astype(jnp.bfloat16)
    low = (table - high.astype(np.float64)).astype(np.float32).astype(jnp.bfloat16)
    return high, low


@functools.cache
def axial_tables():
    points = np.arange(PLANES)[:, None]
    planes = np.arange(PLANES)[None, :]
    mode = np.where(planes == 1, PLANES // 2, planes // 2)
    angles = 2.0 * np.pi / PLANES * ((points * mode) % PLANES)
    sine = (planes % 2 == 1) & (planes != 1)
    basis = np.where(sine, np.sin(angles), np.cos(angles))
    wave = np.where(planes >= 2, mode, 0) * AXIAL_WAVE
    slope = wave * np.where(sine, np.cos(angles), -np.sin(angles))
    weights = np.where(planes <= 1, 1.0 / PLANES, 2.0 / PLANES)
    modal = -np.transpose(weights * basis)
    return halves_np(np.concatenate([basis, slope], axis=0)) + halves_np(modal)


def halves(value):
    high = value.astype(BF16)
    return high, (value - high.astype(F32)).astype(BF16)


def product(left, right):
    return jnp.dot(left, right, preferred_element_type=F32)


def product3(left, right):
    return product(left[0], right[0]) + (product(left[1], right[0]) + product(left[0], right[1]))


def lanes(rows):
    return lax.broadcasted_iota(jnp.int32, (rows, POINTS), 1)


def edge_of(lane):
    return (lane % (EDGES * TRACE)) // TRACE


def call(kernel, outs, *args, flops=0):
    return pl.pallas_call(
        kernel,
        out_shape=[jax.ShapeDtypeStruct(shape, kind) for shape, kind in outs],
        in_specs=[pl.BlockSpec(memory_space=pltpu.VMEM)] * len(args),
        out_specs=[pl.BlockSpec(memory_space=pltpu.VMEM)] * len(outs),
        compiler_params=pltpu.CompilerParams(vmem_limit_bytes=24 * 1024 * 1024),
        cost_estimate=pl.CostEstimate(
            flops=flops or 10**6,
            bytes_accessed=sum(a.size * a.dtype.itemsize for a in args),
            transcendentals=0,
        ),
    )(*args)


def pack_kernel(fields, out):
    for plane in range(OWN):
        for field in range(4):
            out[pl.ds(plane * 4 + field, ELEMS, stride=16), :] = fields[field, plane]


def physical_kernel(fields, factors, flags, deriv, both_h, both_l, modal_h, modal_l, out):
    spectral = jnp.concatenate([fields[pl.ds(c, PLANES, stride=4), :] for c in range(4)], axis=1)
    points = product3((both_h[...], both_l[...]), halves(spectral))
    values = [points[:PLANES, c * POINTS : (c + 1) * POINTS] for c in range(4)]
    first = values[0] * factors[0:1, :]
    second = values[1] * factors[1:2, :]
    third = values[2]
    deriv_halves = halves(deriv[...])
    melting = 1.0 / (1.0 + LATENT * flags[...].astype(F32))
    terms = []
    for c in range(4):
        slopes = product3(halves(values[c]), deriv_halves)
        term = (
            first * slopes[:, :POINTS]
            + second * slopes[:, POINTS:]
            + third * points[PLANES:, c * POINTS : (c + 1) * POINTS]
        )
        terms.append(term * melting if c == 3 else term)
    modal = product3((modal_h[...], modal_l[...]), halves(jnp.concatenate(terms, axis=1)))
    for c in range(4):
        out[pl.ds(c, PLANES, stride=4), :] = modal[:, c * POINTS : (c + 1) * POINTS]


def prepare_kernel(
    weights, edge_back, near, rim_column, rim_row, columns,
    weights_h, weights_l, back_h, back_l, gather, to_rim, from_rim, rim_mask, scale_one, scale_two,
):
    weights_h[...], weights_l[...] = halves(weights[...])
    back_h[...], back_l[...] = halves(edge_back[...])
    wide = lax.broadcasted_iota(jnp.int32, (ROWS, ROWS), 1)
    tall = lax.broadcasted_iota(jnp.int32, (ROWS, ROWS), 0)
    for edge in range(EDGES):
        hit = wide == near[:, edge : edge + 1]
        gather[:, edge * ROWS : (edge + 1) * ROWS] = jnp.where(hit, 1.0, 0.0).astype(BF16)
    to_rim[...] = jnp.where(wide == rim_column[...], 1.0, 0.0).astype(BF16)
    from_rim[...] = jnp.where(tall == rim_row[...], 1.0, 0.0).astype(BF16)
    lane = lanes(ROWS)
    edge = edge_of(lane)
    forward = (edge == 1) & (near[:, 1:2] == -2)
    backward = (edge == 3) & (near[:, 3:4] == -2)
    upper = lane >= EDGES * TRACE
    rim_mask[...] = jnp.where((forward | backward) & upper, 1.0, 0.0)
    scale_one[...] = jnp.broadcast_to(columns[:, 0:1], (ROWS, POINTS))
    scale_two[...] = jnp.broadcast_to(columns[:, 1:2], (ROWS, POINTS))


def two_halves(doubled):
    high = doubled.astype(BF16).astype(F32)
    return jnp.where(lanes(doubled.shape[0]) < EDGES * TRACE, high, doubled - high)


def facing_local(split_traces, gather):
    edge = edge_of(lanes(ROWS))
    stack = [jnp.where(edge == j, split_traces, 0.0).astype(BF16) for j in range(EDGES)]
    return product(gather[...], jnp.concatenate(stack, axis=0))


def start_helmholtz(vector, weights_h, weights_l, back_h, back_l, gather, to_rim, scale_one, scale_two):
    weights = (weights_h[...], weights_l[...])
    images = product3(halves(vector), weights)
    stiff, own, doubled, crossing = (images[:, k * POINTS : (k + 1) * POINTS] for k in range(4))
    traces_split = two_halves(doubled)
    facing = facing_local(traces_split, gather).astype(BF16)
    coupling = product(facing, back_h[...]) + product(facing, back_l[...])
    part = scale_one[...] * vector + scale_two[...] * stiff + own - coupling
    trace_weights = tuple(w[:, 2 * POINTS : 3 * POINTS] for w in weights)
    part_split = two_halves(product3(halves(part), trace_weights))
    rims = product(to_rim[...], jnp.concatenate([traces_split, part_split], axis=1).astype(BF16))
    first, second = rims[:, :POINTS], rims[:, POINTS:]
    first = first + pltpu.roll(first, EDGES * TRACE, 1)
    second = second + pltpu.roll(second, EDGES * TRACE, 1)
    return part, jnp.where(lanes(ROWS) < EDGES * TRACE, first, second), crossing


def first_kernel(
    fields, weights_h, weights_l, back_h, back_l, gather, to_rim, scale_one, scale_two,
    part_out, left_out, right_out,
):
    vector = fields[3].reshape(ROWS, POINTS)
    part, rims, _ = start_helmholtz(
        vector, weights_h, weights_l, back_h, back_l, gather, to_rim, scale_one, scale_two
    )
    part_out[...] = part
    left_out[...] = rims[: OWN * RIM]
    right_out[...] = rims[OWN * RIM :]


def arrived(left, right, from_rim):
    half = OWN * RIM
    edge = edge_of(lanes(half))
    both = jnp.concatenate(
        [jnp.where(edge == 3, left[...], 0.0), jnp.where(edge == 1, right[...], 0.0)], axis=0
    )
    high, low = halves(both)
    spread = product(from_rim[...], jnp.concatenate([high, low], axis=1))
    return spread[:, :POINTS], spread[:, POINTS:]


def rim_coupling(high, low, back_h, back_l):
    lower = lanes(ROWS) < EDGES * TRACE
    high = jnp.where(lower, high, 0.0).astype(BF16)
    low = jnp.where(lower, low, 0.0).astype(BF16)
    return product(high, back_h[...]) + (product(low, back_h[...]) + product(high, back_l[...]))


def base_kernel(fields, part, left, right, from_rim, back_h, back_l, out):
    high, low = arrived(left, right, from_rim)
    image = part[...] - rim_coupling(high, low, back_h, back_l)
    out[...] = INVERSE_STEP * fields[3].reshape(ROWS, POINTS) - image


def residual_kernel(
    modal, base, weights_h, weights_l, back_h, back_l, gather, to_rim, scale_one, scale_two,
    residual_out, part_out, left_out, right_out, crossing_out,
):
    heat = [modal[pl.ds(plane * 4 + 3, ELEMS, stride=16), :] for plane in range(OWN)]
    residual = base[...] + jnp.concatenate(heat, axis=0)
    part, rims, crossing = start_helmholtz(
        residual, weights_h, weights_l, back_h, back_l, gather, to_rim, scale_one, scale_two
    )
    residual_out[...] = residual
    part_out[...] = part
    left_out[...] = rims[: OWN * RIM]
    right_out[...] = rims[OWN * RIM :]
    crossing_out[...] = crossing


def momentum_kernel(modal, out):
    for field in range(3):
        for plane in range(OWN):
            out[field, plane] = modal[pl.ds(plane * 4 + field, ELEMS, stride=16), :]


def moments_kernel(
    residual_ref, part, left, right, crossing, from_rim, weights_h, weights_l, back_h, back_l, gather,
    rim_mask, scale_one, scale_two, image_out, sums_out,
):
    high, low = arrived(left, right, from_rim)
    image = part[...] - rim_coupling(high, low, back_h, back_l)
    image_out[...] = image
    residual = residual_ref[...]
    weights = (
        jnp.concatenate([weights_h[:, :POINTS], weights_h[:, 2 * POINTS : 3 * POINTS]], axis=1),
        jnp.concatenate([weights_l[:, :POINTS], weights_l[:, 2 * POINTS : 3 * POINTS]], axis=1),
    )
    images = product3(halves(image), weights)
    stiff, doubled = images[:, :POINTS], images[:, POINTS:]
    facing = facing_local(two_halves(doubled), gather)
    facing = facing + pltpu.roll(facing, EDGES * TRACE, 1)
    facing = facing + (high + low) - crossing[...] * rim_mask[...]
    own = pltpu.roll(doubled, 2 * TRACE, 1)
    jumps = jnp.where(lanes(ROWS) >= EDGES * TRACE, own * (own - facing), 0.0)
    square = image * image
    cubic = scale_one[...] * square + scale_two[...] * (image * stiff) + jumps
    for number, value in enumerate((residual * residual, residual * image, square, cubic)):
        for plane in range(OWN):
            total = jnp.sum(value[plane * ELEMS : (plane + 1) * ELEMS], axis=0, keepdims=True)
            for peer in range(8):
                row = peer * 16 + number * OWN + plane
                sums_out[row : row + 1, :] = total


def final_kernel(sums, fields, residual, image, out):
    total = sums[0:16, :]
    for peer in range(1, 8):
        total = total + sums[peer * 16 : (peer + 1) * 16, :]
    total = jnp.sum(total, axis=1, keepdims=True)
    m0, m1, m2, m3 = (total[k * OWN : (k + 1) * OWN] for k in range(4))
    step = m0 / m1
    after = m0 + step * (step * m2 - 2.0 * m1)
    after_image = m1 + step * (step * m3 - 2.0 * m2)
    ratio = after / m0
    second = after / (after_image - ratio * after / step)
    on_residual = step + second * (1.0 + ratio)
    on_image = -second * step
    for plane in range(OWN):
        rows = pl.ds(plane * ELEMS, ELEMS)
        out[plane] = (
            fields[3, plane]
            + on_residual[plane : plane + 1] * residual[rows, :]
            + on_image[plane : plane + 1] * image[rows, :]
        )


def per_device(
    spectral_fields,
    deriv_ops,
    geom,
    stiffness,
    stiff_scale,
    traces,
    neighbors,
    rim_lists,
    melt_flags,
):
    highest = lax.Precision.HIGHEST
    plane_rank = lax.axis_index("plane")
    dom_rank = lax.axis_index("dom")
    count = lax.axis_size("dom")
    groups = lax.axis_size("plane")
    whole = ((ROWS, POINTS), F32)
    rims = ((OWN * RIM, POINTS), F32)

    with jax.named_scope("to_points"):
        (packed,) = call(pack_kernel, [((ELEMS * 16, POINTS), F32)], spectral_fields)
        gathered = lax.all_to_all(
            packed.reshape(groups, 16, POINTS), "plane", split_axis=0, concat_axis=0, tiled=True
        ).reshape(groups * 16, POINTS)

    with jax.named_scope("operator_tables"):
        edges = traces.reshape(EDGES * TRACE, POINTS)
        turned = jnp.concatenate([edges[2 * TRACE :], edges[: 2 * TRACE]], axis=0)
        own = jnp.dot(edges.T, edges, precision=highest)
        square_one = jnp.dot(traces[1], traces[1].T, precision=highest)
        square_three = jnp.dot(traces[3], traces[3].T, precision=highest)
        empty = jnp.zeros((POINTS, TRACE), F32)
        crossing = jnp.concatenate(
            [
                empty,
                jnp.dot(traces[1].T, square_three, precision=highest),
                empty,
                jnp.dot(traces[3].T, square_one, precision=highest),
            ],
            axis=1,
        )
        weights = jnp.concatenate(
            [stiffness, own, turned.T, turned.T, jnp.zeros((POINTS, EDGES * TRACE), F32), crossing],
            axis=1,
        )
        edge_back = jnp.concatenate([edges, edges], axis=0)
        shift = (jnp.arange(OWN, dtype=jnp.int32) * ELEMS)[:, None]
        local = jnp.where(neighbors >= 0, neighbors - dom_rank * ELEMS, neighbors)
        near = jnp.where(local[None] >= 0, local[None] + shift[:, :, None], local[None]).reshape(ROWS, EDGES)
        rim = (rim_lists[0][:, None, :] + shift[None]).reshape(2 * OWN * RIM)
        wave = (plane_rank * OWN + jnp.arange(OWN)).astype(jnp.int32)
        wave = jnp.where(wave == 1, PLANES // 2, wave // 2).astype(F32) * AXIAL_WAVE
        columns = jnp.stack(
            [jnp.repeat(INVERSE_STEP + wave**2, ELEMS), jnp.tile(stiff_scale, OWN)], axis=1
        )
        (
            weights_h, weights_l, back_h, back_l, gather, to_rim, from_rim, rim_mask, scale_one, scale_two,
        ) = call(
            prepare_kernel,
            [
                ((POINTS, 4 * POINTS), BF16),
                ((POINTS, 4 * POINTS), BF16),
                ((POINTS, POINTS), BF16),
                ((POINTS, POINTS), BF16),
                ((ROWS, EDGES * ROWS), BF16),
                ((ROWS, ROWS), BF16),
                ((ROWS, ROWS), BF16),
                whole,
                whole,
                whole,
            ],
            weights,
            edge_back,
            near,
            rim[:, None],
            rim[None, :],
            columns,
        )
        tables = (weights_h, weights_l, back_h, back_l, gather, to_rim, scale_one, scale_two)

    def exchange(left, right):
        from_left = lax.ppermute(right, "dom", [(i, (i + 1) % count) for i in range(count)])
        from_right = lax.ppermute(left, "dom", [((i + 1) % count, i) for i in range(count)])
        return from_left, from_right

    with jax.named_scope("base"):
        part, left, right = call(first_kernel, [whole, rims, rims], spectral_fields, *tables)
        left, right = exchange(left, right)
        (base,) = call(
            base_kernel, [whole], spectral_fields, part, left, right, from_rim, back_h, back_l
        )

    with jax.named_scope("advection"):
        factors = lax.dynamic_slice_in_dim(geom, plane_rank, 1, axis=1)[:, 0]
        deriv = jnp.concatenate([deriv_ops[0].T, deriv_ops[1].T], axis=1)
        (modal,) = call(
            physical_kernel,
            [((groups * 16, POINTS), F32)],
            gathered,
            factors,
            melt_flags,
            deriv,
            *(jnp.asarray(t) for t in axial_tables()),
            flops=10**9,
        )
        returned = lax.all_to_all(
            modal.reshape(groups, 16, POINTS), "plane", split_axis=0, concat_axis=0, tiled=True
        ).reshape(ELEMS * 16, POINTS)

    with jax.named_scope("solve"):
        residual, part, left, right, crossing_part = call(
            residual_kernel, [whole, whole, rims, rims, whole], returned, base, *tables
        )
        left, right = exchange(left, right)
        (momentum,) = call(momentum_kernel, [((3, OWN, ELEMS, POINTS), F32)], returned)
        image, sums = call(
            moments_kernel,
            [whole, ((8 * 16, POINTS), F32)],
            residual,
            part,
            left,
            right,
            crossing_part,
            from_rim,
            weights_h,
            weights_l,
            back_h,
            back_l,
            gather,
            rim_mask,
            scale_one,
            scale_two,
        )
        sums = lax.all_to_all(
            sums.reshape(8, 16, POINTS), "dom", split_axis=0, concat_axis=0, tiled=True
        ).reshape(8 * 16, POINTS)
        (temperature,) = call(
            final_kernel, [((OWN, ELEMS, POINTS), F32)], sums, spectral_fields, residual, image
        )
    return momentum, temperature


def solution(mesh):
    placed = (
        P(None, "plane", "dom", None),
        P(),
        P(None, "dom", None),
        P(),
        P("dom"),
        P(),
        P("dom", None),
        P("dom", None, None),
        P(None, ("dom", "plane")),
    )
    return jax.shard_map(
        per_device,
        mesh=mesh,
        in_specs=placed,
        out_specs=(P(None, "plane", "dom", None), P("plane", "dom", None)),
        check_vma=False,
    )
```

```python
import functools

import jax
import jax.numpy as jnp
import numpy as np
from jax import lax
from jax.experimental import pallas as pl
from jax.experimental.pallas import tpu as pltpu
from jax.sharding import PartitionSpec as P

PLANES = 256
POINTS = 128
ELEMS = 64
OWN = 4
EDGES = 4
TRACE = 16
RIM = 32
ROWS = OWN * ELEMS
AXIAL_WAVE = 0.01
INVERSE_STEP = 0.5
LATENT = 2.0
F32 = jnp.float32
BF16 = jnp.bfloat16


def halves_np(table):
    high = table.astype(np.float32).astype(jnp.bfloat16)
    low = (table - high.astype(np.float64)).astype(np.float32).astype(jnp.bfloat16)
    return high, low


@functools.cache
def axial_tables():
    points = np.arange(PLANES)[:, None]
    planes = np.arange(PLANES)[None, :]
    mode = np.where(planes == 1, PLANES // 2, planes // 2)
    angles = 2.0 * np.pi / PLANES * ((points * mode) % PLANES)
    sine = (planes % 2 == 1) & (planes != 1)
    basis = np.where(sine, np.sin(angles), np.cos(angles))
    wave = np.where(planes >= 2, mode, 0) * AXIAL_WAVE
    slope = wave * np.where(sine, np.cos(angles), -np.sin(angles))
    weights = np.where(planes <= 1, 1.0 / PLANES, 2.0 / PLANES)
    modal = -np.transpose(weights * basis)
    both_h, both_l = halves_np(np.concatenate([basis, slope], axis=0))
    modal_h, modal_l = halves_np(modal)
    return np.concatenate([both_h, both_l, modal_h, modal_l], axis=0)


def halves(value):
    high = value.astype(BF16)
    return high, (value - high.astype(F32)).astype(BF16)


def product(left, right):
    return jnp.dot(left, right, preferred_element_type=F32)


def product3(left, right):
    return product(left[0], right[0]) + (product(left[1], right[0]) + product(left[0], right[1]))


def lanes(rows):
    return lax.broadcasted_iota(jnp.int32, (rows, POINTS), 1)


def edge_of(lane):
    return (lane % (EDGES * TRACE)) // TRACE


def call(kernel, outs, *args, flops=0, specs=None):
    return pl.pallas_call(
        kernel,
        grid=(1,) if specs else (),
        out_shape=[jax.ShapeDtypeStruct(shape, kind) for shape, kind in outs],
        in_specs=specs or [pl.BlockSpec(memory_space=pltpu.VMEM)] * len(args),
        out_specs=[pl.BlockSpec(memory_space=pltpu.VMEM)] * len(outs),
        compiler_params=pltpu.CompilerParams(vmem_limit_bytes=24 * 1024 * 1024),
        cost_estimate=pl.CostEstimate(
            flops=flops or 10**7,
            bytes_accessed=sum(a.size * a.dtype.itemsize for a in args),
            transcendentals=0,
        ),
    )(*args)


def stacked(value):
    return jnp.concatenate(halves(value), axis=1)


def product_stacked(value, twice_h, low):
    pair = stacked(value)
    return product(pair, twice_h) + product(pair[:, : low.shape[0]], low)


def pack_kernel(fields, out):
    for plane in range(OWN):
        for field in range(4):
            out[pl.ds(plane * 4 + field, ELEMS, stride=16), :] = fields[field, plane]


def physical_kernel(fields, factors, melting, deriv_h, deriv_l, tables, out):
    spectral = jnp.concatenate([fields[pl.ds(c, PLANES, stride=4), :] for c in range(4)], axis=1)
    both_h, both_l, modal_h, modal_l = (
        tables[start : start + size]
        for start, size in ((0, 512), (512, 512), (1024, 256), (1280, 256))
    )
    points = product3((both_h, both_l), halves(spectral))
    values = [points[:PLANES, c * POINTS : (c + 1) * POINTS] for c in range(4)]
    first = values[0] * factors[0:1, :]
    second = values[1] * factors[1:2, :]
    third = values[2]
    terms = []
    for c in range(4):
        slopes = product_stacked(values[c], deriv_h[...], deriv_l[...])
        term = (
            first * slopes[:, :POINTS]
            + second * slopes[:, POINTS:]
            + third * points[PLANES:, c * POINTS : (c + 1) * POINTS]
        )
        terms.append(term * melting[...] if c == 3 else term)
    modal = product3((modal_h, modal_l), halves(jnp.concatenate(terms, axis=1)))
    for c in range(4):
        out[pl.ds(c, PLANES, stride=4), :] = modal[:, c * POINTS : (c + 1) * POINTS]


def upright(row):
    size = row.shape[1]
    down = lax.broadcasted_iota(jnp.int32, (size, size), 0)
    along = lax.broadcasted_iota(jnp.int32, (size, size), 1)
    return jnp.sum(jnp.where(down == along, row, 0.0), axis=1, keepdims=True)


def exact(left, right):
    return jnp.dot(left, right, preferred_element_type=F32, precision=lax.Precision.HIGHEST)


def two_halves(doubled):
    high = doubled.astype(BF16).astype(F32)
    return jnp.where(lanes(doubled.shape[0]) < EDGES * TRACE, high, doubled - high)


def facing_local(split_traces, gather):
    edge = edge_of(lanes(ELEMS))
    parts = []
    for plane in range(OWN):
        own = split_traces[plane * ELEMS : (plane + 1) * ELEMS]
        stack = [jnp.where(edge == j, own, 0.0).astype(BF16) for j in range(EDGES)]
        parts.append(product(gather, jnp.concatenate(stack, axis=0)))
    return jnp.concatenate(parts, axis=0)


def packed_rims(rims, edge):
    lane = lanes(RIM)
    total = jnp.zeros((RIM, POINTS), F32)
    for plane in range(OWN):
        rows = rims[plane * RIM : (plane + 1) * RIM]
        for which in range(2):
            at = plane * 2 * TRACE + which * TRACE
            moved = pltpu.roll(rows, (at - which * EDGES * TRACE - edge * TRACE) % POINTS, 1)
            total = jnp.where((lane >= at) & (lane < at + TRACE), moved, total)
    return total


def unpacked_rims(packed, edge):
    lane = lanes(RIM)
    parts = []
    for plane in range(OWN):
        total = jnp.zeros((RIM, POINTS), F32)
        for which in range(2):
            at = which * EDGES * TRACE + edge * TRACE
            moved = pltpu.roll(packed, (at - plane * 2 * TRACE - which * TRACE) % POINTS, 1)
            total = jnp.where((lane >= at) & (lane < at + TRACE), moved, total)
        parts.append(total)
    return jnp.concatenate(parts, axis=0)


def doubled_sum(value):
    return value + pltpu.roll(value, EDGES * TRACE, 1)


def start_helmholtz(vector, weights_h, weights_l, back, gather, to_rim, scale_one, scale_two):
    images = product_stacked(vector, weights_h, weights_l)
    stiff, own, doubled, crossing, stiff_trace, own_trace = (
        images[:, k * POINTS : (k + 1) * POINTS] for k in range(6)
    )
    traces_split = two_halves(doubled)
    facing = facing_local(traces_split, gather).astype(BF16)
    coupling = product(jnp.concatenate([facing, facing], axis=1), back)
    part = scale_one * vector + scale_two * stiff + own - coupling[:, :POINTS]
    part_trace = scale_one * doubled + scale_two * stiff_trace + own_trace - coupling[:, POINTS:]
    split = jnp.concatenate([traces_split, two_halves(part_trace)], axis=1).astype(BF16)
    rims = product(to_rim, split)
    first, second = doubled_sum(rims[:, :POINTS]), doubled_sum(rims[:, POINTS:])
    rims = jnp.where(lanes(ROWS) < EDGES * TRACE, first, second)
    half = OWN * RIM
    return part, packed_rims(rims[:half], 1), packed_rims(rims[half:], 3), crossing


def arrived(left, right, from_rim):
    both = jnp.concatenate([unpacked_rims(left[...], 3), unpacked_rims(right[...], 1)], axis=0)
    spread = product(from_rim[...], stacked(both))
    return spread[:, :POINTS], spread[:, POINTS:]


def rim_coupling(high, low, back):
    facing = jnp.where(
        lanes(ROWS) < EDGES * TRACE, high, pltpu.roll(low, EDGES * TRACE, 1)
    ).astype(BF16)
    return product(jnp.concatenate([facing, facing], axis=1), back[:, :POINTS])


def prepare_kernel(
    stiffness, traces, scale_row, near_rows, rim_rows, flags, deriv, geom, fields,
    weights_h, weights_l, back, gather, to_rim, from_rim, rim_mask, scale_one, scale_two,
    melting, factors, deriv_h, deriv_l, part_out, left_out, right_out,
):
    plane_rank = lax.axis_index("plane")
    dom_rank = lax.axis_index("dom")
    edges = traces[...].reshape(EDGES * TRACE, POINTS)
    turned = jnp.concatenate([edges[2 * TRACE :], edges[: 2 * TRACE]], axis=0)
    edges = jnp.concatenate([edges, edges], axis=0)
    turned = jnp.concatenate([turned, turned], axis=0)
    edges_up = jnp.transpose(edges)
    turned_up = jnp.transpose(turned)
    stiff = stiffness[...]
    own = 0.5 * exact(edges_up, edges)
    down = lax.broadcasted_iota(jnp.int32, (POINTS, POINTS), 0)
    along = lanes(POINTS)
    lower = EDGES * TRACE
    kept = (
        (down < lower)
        & (along >= lower)
        & (edge_of(down) == edge_of(along))
        & (edge_of(along) % 2 == 1)
    )
    crossing = exact(edges_up, jnp.where(kept, exact(turned, turned_up), 0.0))
    weights = jnp.concatenate(
        [stiff, own, turned_up, crossing, exact(stiff, turned_up), exact(own, turned_up)], axis=1
    )
    high, low = halves(weights)
    weights_h[...] = jnp.concatenate([high, high], axis=0)
    weights_l[...] = low
    high, low = halves(jnp.concatenate([edges, exact(edges, turned_up)], axis=1))
    back[...] = jnp.concatenate([high, low], axis=0)

    rows = near_rows[...]
    rows = jnp.where(rows >= 0, rows - dom_rank * ELEMS, rows).astype(F32)
    near = [upright(rows[edge : edge + 1]).astype(jnp.int32) for edge in range(EDGES)]
    cell = lax.broadcasted_iota(jnp.int32, (ELEMS, EDGES * ELEMS), 1)
    wanted = near[EDGES - 1]
    for edge in range(EDGES - 1):
        wanted = jnp.where(cell // ELEMS == edge, near[edge], wanted)
    gather[...] = jnp.where(cell % ELEMS == wanted, 1.0, 0.0).astype(BF16)
    wide = lax.broadcasted_iota(jnp.int32, (ROWS, ROWS), 1)
    rims = [upright(rim_rows[side : side + 1, :].astype(F32)).astype(jnp.int32) for side in range(2)]
    column = jnp.concatenate([rims[side] + plane * ELEMS for side in range(2) for plane in range(OWN)], axis=0)
    picked = jnp.where(wide == column, 1.0, 0.0)
    to_rim[...] = picked.astype(BF16)
    from_rim[...] = jnp.transpose(picked).astype(BF16)
    lane = lanes(ELEMS)
    edge = edge_of(lane)
    beyond = ((edge == 1) & (near[1] == -2)) | ((edge == 3) & (near[3] == -2))
    mask = jnp.where(beyond & (lane >= lower), 1.0, 0.0)
    scale = jnp.broadcast_to(upright(scale_row[...]), (ELEMS, POINTS))
    plane = plane_rank * OWN + lax.broadcasted_iota(jnp.int32, (ROWS, POINTS), 0) // ELEMS
    wave = jnp.where(plane == 1, PLANES // 2, plane // 2).astype(F32) * AXIAL_WAVE
    one = INVERSE_STEP + wave * wave
    two = jnp.concatenate([scale] * OWN, axis=0)
    rim_mask[...] = jnp.concatenate([mask] * OWN, axis=0)
    scale_one[...] = one
    scale_two[...] = two

    melted = upright(flags[...].astype(F32))
    melting[...] = jnp.broadcast_to(1.0 / (1.0 + LATENT * melted), (PLANES, POINTS))
    for side in range(2):
        factors[side : side + 1, :] = geom[side, pl.ds(plane_rank, 1), :]
    high, low = halves(jnp.concatenate([jnp.transpose(deriv[0]), jnp.transpose(deriv[1])], axis=1))
    deriv_h[...] = jnp.concatenate([high, high], axis=0)
    deriv_l[...] = low

    vector = fields[0].reshape(ROWS, POINTS)
    part, left, right, _ = start_helmholtz(
        vector, weights_h[...], weights_l[...], back[...], gather[...], to_rim[...], one, two
    )
    part_out[...] = part
    left_out[...] = left
    right_out[...] = right


def base_kernel(fields, part, left, right, from_rim, back, out):
    high, low = arrived(left, right, from_rim)
    image = part[...] - rim_coupling(high, low, back[...])
    out[...] = INVERSE_STEP * fields[0].reshape(ROWS, POINTS) - image


def residual_kernel(
    modal, base, weights_h, weights_l, back, gather, to_rim, scale_one, scale_two,
    residual_out, part_out, left_out, right_out, crossing_out,
):
    heat = [modal[pl.ds(plane * 4 + 3, ELEMS, stride=16), :] for plane in range(OWN)]
    residual = base[...] + jnp.concatenate(heat, axis=0)
    part, left, right, crossing = start_helmholtz(
        residual,
        weights_h[...],
        weights_l[...],
        back[...],
        gather[...],
        to_rim[...],
        scale_one[...],
        scale_two[...],
    )
    left_out[...] = left
    right_out[...] = right
    residual_out[...] = residual
    part_out[...] = part
    crossing_out[...] = crossing


def momentum_kernel(modal, out):
    for field in range(3):
        for plane in range(OWN):
            out[field, plane] = modal[pl.ds(plane * 4 + field, ELEMS, stride=16), :]


def moments_kernel(
    residual_ref, part, left, right, crossing, from_rim, weights_h, weights_l, back, gather,
    rim_mask, scale_one, scale_two, image_out, sums_out,
):
    high, low = arrived(left, right, from_rim)
    image = part[...] - rim_coupling(high, low, back[...])
    image_out[...] = image
    residual = residual_ref[...]
    weights = [
        jnp.concatenate([w[:, :POINTS], w[:, 2 * POINTS : 3 * POINTS]], axis=1)
        for w in (weights_h, weights_l)
    ]
    images = product_stacked(image, *weights)
    stiff, doubled = images[:, :POINTS], images[:, POINTS:]
    facing = doubled_sum(facing_local(two_halves(doubled), gather[...]))
    facing = facing + (high + low) - crossing[...] * rim_mask[...]
    own = pltpu.roll(doubled, 2 * TRACE, 1)
    jumps = jnp.where(lanes(ROWS) >= EDGES * TRACE, own * (own - facing), 0.0)
    square = image * image
    cubic = scale_one[...] * square + scale_two[...] * (image * stiff) + jumps
    for number, value in enumerate((residual * residual, residual * image, square, cubic)):
        for plane in range(OWN):
            total = jnp.sum(value[plane * ELEMS : (plane + 1) * ELEMS], axis=0, keepdims=True)
            for peer in range(8):
                row = peer * 16 + number * OWN + plane
                sums_out[row : row + 1, :] = total


def final_kernel(sums, fields, residual, image, out):
    total = sums[0:16, :]
    for peer in range(1, 8):
        total = total + sums[peer * 16 : (peer + 1) * 16, :]
    total = jnp.sum(total, axis=1, keepdims=True)
    m0, m1, m2, m3 = (total[k * OWN : (k + 1) * OWN] for k in range(4))
    step = m0 / m1
    after = m0 + step * (step * m2 - 2.0 * m1)
    after_image = m1 + step * (step * m3 - 2.0 * m2)
    ratio = after / m0
    second = after / (after_image - ratio * after / step)
    on_residual = step + second * (1.0 + ratio)
    on_image = -second * step
    for plane in range(OWN):
        rows = pl.ds(plane * ELEMS, ELEMS)
        out[plane] = (
            fields[0, plane]
            + on_residual[plane : plane + 1] * residual[rows, :]
            + on_image[plane : plane + 1] * image[rows, :]
        )


def per_device(
    spectral_fields,
    deriv_ops,
    geom,
    stiffness,
    stiff_scale,
    traces,
    neighbors,
    rim_lists,
    melt_flags,
):
    count = lax.axis_size("dom")
    groups = lax.axis_size("plane")
    whole = ((ROWS, POINTS), F32)
    rims = ((RIM, POINTS), F32)
    plain = pl.BlockSpec(memory_space=pltpu.VMEM)
    heat_only = pl.BlockSpec((1, OWN, ELEMS, POINTS), lambda *_: (3, 0, 0, 0), memory_space=pltpu.VMEM)

    with jax.named_scope("to_points"):
        (packed,) = call(pack_kernel, [((ELEMS * 16, POINTS), F32)], spectral_fields)
        gathered = lax.all_to_all(
            packed.reshape(groups, 16, POINTS), "plane", split_axis=0, concat_axis=0, tiled=True
        ).reshape(groups * 16, POINTS)

    def exchange(left, right):
        from_left = lax.ppermute(right, "dom", [(i, (i + 1) % count) for i in range(count)])
        from_right = lax.ppermute(left, "dom", [((i + 1) % count, i) for i in range(count)])
        return from_left, from_right

    with jax.named_scope("base"):
        (
            weights_h, weights_l, back, gather, to_rim, from_rim, rim_mask, scale_one, scale_two,
            melting, factors, deriv_h, deriv_l, part, left, right,
        ) = call(
            prepare_kernel,
            [
                ((2 * POINTS, 6 * POINTS), BF16),
                ((POINTS, 6 * POINTS), BF16),
                ((2 * POINTS, 2 * POINTS), BF16),
                ((ELEMS, EDGES * ELEMS), BF16),
                ((ROWS, ROWS), BF16),
                ((ROWS, ROWS), BF16),
                whole,
                whole,
                whole,
                whole,
                ((2, POINTS), F32),
                ((2 * POINTS, 2 * POINTS), BF16),
                ((POINTS, 2 * POINTS), BF16),
                whole,
                rims,
                rims,
            ],
            stiffness,
            traces,
            stiff_scale.reshape(1, ELEMS),
            neighbors.T,
            rim_lists[0],
            melt_flags.reshape(1, PLANES),
            deriv_ops,
            geom,
            spectral_fields,
            specs=[plain] * 8 + [heat_only],
        )
        left, right = exchange(left, right)
        (base,) = call(
            base_kernel,
            [whole],
            spectral_fields,
            part,
            left,
            right,
            from_rim,
            back,
            specs=[heat_only] + [plain] * 5,
        )

    with jax.named_scope("advection"):
        gathered, base = lax.optimization_barrier((gathered, base))
        (modal,) = call(
            physical_kernel,
            [((groups * 16, POINTS), F32)],
            gathered,
            factors,
            melting,
            deriv_h,
            deriv_l,
            jnp.asarray(axial_tables()),
            flops=10**9,
        )
        returned = lax.all_to_all(
            modal.reshape(groups, 16, POINTS), "plane", split_axis=0, concat_axis=0, tiled=True
        ).reshape(ELEMS * 16, POINTS)

    with jax.named_scope("solve"):
        residual, part, left, right, crossing = call(
            residual_kernel,
            [whole, whole, rims, rims, whole],
            returned,
            base,
            weights_h,
            weights_l,
            back,
            gather,
            to_rim,
            scale_one,
            scale_two,
        )
        left, right = exchange(left, right)
        (momentum,) = call(momentum_kernel, [((3, OWN, ELEMS, POINTS), F32)], returned)
        left, right, momentum = lax.optimization_barrier((left, right, momentum))
        image, sums = call(
            moments_kernel,
            [whole, ((8 * 16, POINTS), F32)],
            residual,
            part,
            left,
            right,
            crossing,
            from_rim,
            weights_h,
            weights_l,
            back,
            gather,
            rim_mask,
            scale_one,
            scale_two,
        )
        sums = lax.all_to_all(
            sums.reshape(8, 16, POINTS), "dom", split_axis=0, concat_axis=0, tiled=True
        ).reshape(8 * 16, POINTS)
        (temperature,) = call(
            final_kernel,
            [((OWN, ELEMS, POINTS), F32)],
            sums,
            spectral_fields,
            residual,
            image,
            specs=[plain, heat_only, plain, plain],
        )
    return momentum, temperature


def solution(mesh):
    placed = (
        P(None, "plane", "dom", None),
        P(),
        P(None, "dom", None),
        P(),
        P("dom"),
        P(),
        P("dom", None),
        P("dom", None, None),
        P(None, ("dom", "plane")),
    )
    return jax.shard_map(
        per_device,
        mesh=mesh,
        in_specs=placed,
        out_specs=(P(None, "plane", "dom", None), P("plane", "dom", None)),
        check_vma=False,
    )
```

```python
import functools

import jax
import jax.numpy as jnp
import numpy as np
from jax import lax
from jax.experimental import pallas as pl
from jax.experimental.pallas import tpu as pltpu
from jax.sharding import PartitionSpec as P

PLANES = 256
POINTS = 128
ELEMS = 64
OWN = 4
EDGES = 4
TRACE = 16
RIM = 32
ROWS = OWN * ELEMS
AXIAL_WAVE = 0.01
INVERSE_STEP = 0.5
LATENT = 2.0
F32 = jnp.float32
BF16 = jnp.bfloat16


def halves_np(table):
    high = table.astype(np.float32).astype(jnp.bfloat16)
    low = (table - high.astype(np.float64)).astype(np.float32).astype(jnp.bfloat16)
    return high, low


@functools.cache
def axial_table():
    points = np.arange(PLANES)[:, None]
    modes = np.arange(PLANES // 2)[None, :]
    angles = 2.0 * np.pi / PLANES * ((points * modes) % PLANES)
    others = np.where(modes == 0, 1.0 - 2.0 * (points % 2), np.sin(angles))
    return np.concatenate(halves_np(np.concatenate([np.cos(angles), others], axis=1)), axis=0)


def halves(value):
    high = value.astype(BF16)
    return high, (value - high.astype(F32)).astype(BF16)


def product(left, right):
    return jnp.dot(left, right, preferred_element_type=F32)


def across(left, right):
    return lax.dot_general(left, right, (((0,), (0,)), ((), ())), preferred_element_type=F32)


def product3(left, right):
    return product(left[0], right[0]) + (product(left[1], right[0]) + product(left[0], right[1]))


def lanes(rows):
    return lax.broadcasted_iota(jnp.int32, (rows, POINTS), 1)


def edge_of(lane):
    return (lane % (EDGES * TRACE)) // TRACE


def call(kernel, outs, *args, flops=0, specs=None):
    return pl.pallas_call(
        kernel,
        grid=(1,) if specs else (),
        out_shape=[jax.ShapeDtypeStruct(shape, kind) for shape, kind in outs],
        in_specs=specs or [pl.BlockSpec(memory_space=pltpu.VMEM)] * len(args),
        out_specs=[pl.BlockSpec(memory_space=pltpu.VMEM)] * len(outs),
        compiler_params=pltpu.CompilerParams(vmem_limit_bytes=24 * 1024 * 1024),
        cost_estimate=pl.CostEstimate(
            flops=flops or 10**7,
            bytes_accessed=sum(a.size * a.dtype.itemsize for a in args),
            transcendentals=0,
        ),
    )(*args)


def stacked(value):
    return jnp.concatenate(halves(value), axis=1)


def product_stacked(value, high, low):
    pair = stacked(value)
    twice = jnp.concatenate([high, high], axis=0)
    return product(pair, twice) + product(pair[:, : low.shape[0]], low)


def pack_kernel(fields, out):
    for plane in range(OWN):
        for field in range(4):
            out[pl.ds(plane * 4 + field, ELEMS, stride=16), :] = fields[field, plane]


def physical_kernel(fields, factors, melting, deriv_h, deriv_l, table, out):
    half = PLANES // 2
    even = [fields[pl.ds(c, half, stride=8), :] for c in range(4)]
    odd = [fields[pl.ds(4 + c, half, stride=8), :] for c in range(4)]
    even, odd = jnp.concatenate(even, axis=1), jnp.concatenate(odd, axis=1)
    mode = lax.broadcasted_iota(jnp.int32, (half, 4 * POINTS), 0)
    wave = mode.astype(F32) * AXIAL_WAVE
    spectral = jnp.concatenate(
        [jnp.concatenate([even, wave * odd], axis=1), jnp.concatenate([odd, -wave * even], axis=1)], axis=0
    )
    basis = (table[:PLANES], table[PLANES:])
    points = product3(basis, halves(spectral))
    values = [points[:, c * POINTS : (c + 1) * POINTS] for c in range(4)]
    axial = [points[:, c * POINTS : (c + 1) * POINTS] for c in range(4, 8)]
    first = values[0] * factors[0:1, :]
    second = values[1] * factors[1:2, :]
    third = values[2]
    terms = []
    for c in range(4):
        slopes = product_stacked(values[c], deriv_h[...], deriv_l[...])
        term = first * slopes[:, :POINTS] + second * slopes[:, POINTS:] + third * axial[c]
        terms.append(term * melting[...] if c == 3 else term)
    terms = halves(jnp.concatenate(terms, axis=1))
    modal = across(basis[0], terms[0]) + (across(basis[1], terms[0]) + across(basis[0], terms[1]))
    row = lax.broadcasted_iota(jnp.int32, (PLANES, 4 * POINTS), 0)
    modal = modal * jnp.where(row % half == 0, -1.0 / PLANES, -2.0 / PLANES)
    for c in range(4):
        out[pl.ds(c, half, stride=8), :] = modal[:half, c * POINTS : (c + 1) * POINTS]
        out[pl.ds(4 + c, half, stride=8), :] = modal[half:, c * POINTS : (c + 1) * POINTS]


def upright(row):
    size = row.shape[1]
    down = lax.broadcasted_iota(jnp.int32, (size, size), 0)
    along = lax.broadcasted_iota(jnp.int32, (size, size), 1)
    return jnp.sum(jnp.where(down == along, row, 0.0), axis=1, keepdims=True)


def exact(left, right):
    return jnp.dot(left, right, preferred_element_type=F32, precision=lax.Precision.HIGHEST)


def two_halves(doubled):
    high = doubled.astype(BF16).astype(F32)
    return jnp.where(lanes(doubled.shape[0]) < EDGES * TRACE, high, doubled - high)


def facing_local(split_traces, gather):
    edge = edge_of(lanes(ELEMS))
    parts = []
    for plane in range(OWN):
        own = split_traces[plane * ELEMS : (plane + 1) * ELEMS]
        stack = [jnp.where(edge == j, own, 0.0).astype(BF16) for j in range(EDGES)]
        parts.append(product(gather, jnp.concatenate(stack, axis=0)))
    return jnp.concatenate(parts, axis=0)


def packed_rims(rims, edge):
    lane = lanes(RIM)
    total = jnp.zeros((RIM, POINTS), F32)
    for plane in range(OWN):
        rows = rims[plane * RIM : (plane + 1) * RIM]
        for which in range(2):
            at = plane * 2 * TRACE + which * TRACE
            moved = pltpu.roll(rows, (at - which * EDGES * TRACE - edge * TRACE) % POINTS, 1)
            total = jnp.where((lane >= at) & (lane < at + TRACE), moved, total)
    return total


def unpacked_rims(packed, edge):
    lane = lanes(RIM)
    parts = []
    for plane in range(OWN):
        total = jnp.zeros((RIM, POINTS), F32)
        for which in range(2):
            at = which * EDGES * TRACE + edge * TRACE
            moved = pltpu.roll(packed, (at - plane * 2 * TRACE - which * TRACE) % POINTS, 1)
            total = jnp.where((lane >= at) & (lane < at + TRACE), moved, total)
        parts.append(total)
    return jnp.concatenate(parts, axis=0)


def doubled_sum(value):
    return value + pltpu.roll(value, EDGES * TRACE, 1)


def by_plane(rows):
    return jnp.concatenate(
        [jnp.broadcast_to(rows[plane : plane + 1], (ELEMS, POINTS)) for plane in range(OWN)], axis=0
    )


def by_element(rows):
    return jnp.concatenate([rows] * OWN, axis=0)


def start_helmholtz(vector, weights_h, weights_l, back, gather, to_rim, scale_one, scale_two):
    scale_one, scale_two = by_plane(scale_one), by_element(scale_two)
    images = product_stacked(vector, weights_h, weights_l)
    stiff, own, doubled, crossing, stiff_trace, own_trace = (
        images[:, k * POINTS : (k + 1) * POINTS] for k in range(6)
    )
    traces_split = two_halves(doubled)
    facing = facing_local(traces_split, gather).astype(BF16)
    coupling = product(jnp.concatenate([facing, facing], axis=1), back)
    part = scale_one * vector + scale_two * stiff + own - coupling[:, :POINTS]
    part_trace = scale_one * doubled + scale_two * stiff_trace + own_trace - coupling[:, POINTS:]
    split = jnp.concatenate([traces_split, two_halves(part_trace)], axis=1).astype(BF16)
    rims = product(to_rim, split)
    first, second = doubled_sum(rims[:, :POINTS]), doubled_sum(rims[:, POINTS:])
    rims = jnp.where(lanes(ROWS) < EDGES * TRACE, first, second)
    half = OWN * RIM
    return part, packed_rims(rims[:half], 1), packed_rims(rims[half:], 3), crossing


def arrived(left, right, from_rim):
    both = jnp.concatenate([unpacked_rims(left[...], 3), unpacked_rims(right[...], 1)], axis=0)
    spread = product(from_rim[...], stacked(both))
    return spread[:, :POINTS], spread[:, POINTS:]


def rim_coupling(high, low, back):
    facing = jnp.where(
        lanes(ROWS) < EDGES * TRACE, high, pltpu.roll(low, EDGES * TRACE, 1)
    ).astype(BF16)
    return product(jnp.concatenate([facing, facing], axis=1), back[:, :POINTS])


def prepare_kernel(
    stiffness, traces, scale_row, near_rows, rim_rows, flags, deriv, geom, fields,
    weights_h, weights_l, back, gather, to_rim, from_rim, rim_mask, scale_one, scale_two,
    melting, factors, deriv_h, deriv_l, part_out, left_out, right_out,
):
    plane_rank = lax.axis_index("plane")
    dom_rank = lax.axis_index("dom")
    edges = traces[...].reshape(EDGES * TRACE, POINTS)
    turned = jnp.concatenate([edges[2 * TRACE :], edges[: 2 * TRACE]], axis=0)
    edges = jnp.concatenate([edges, edges], axis=0)
    turned = jnp.concatenate([turned, turned], axis=0)
    edges_up = jnp.transpose(edges)
    turned_up = jnp.transpose(turned)
    stiff = stiffness[...]
    own = 0.5 * exact(edges_up, edges)
    down = lax.broadcasted_iota(jnp.int32, (POINTS, POINTS), 0)
    along = lanes(POINTS)
    lower = EDGES * TRACE
    kept = (
        (down < lower)
        & (along >= lower)
        & (edge_of(down) == edge_of(along))
        & (edge_of(along) % 2 == 1)
    )
    crossing = exact(edges_up, jnp.where(kept, exact(turned, turned_up), 0.0))
    weights = jnp.concatenate(
        [stiff, own, turned_up, crossing, exact(stiff, turned_up), exact(own, turned_up)], axis=1
    )
    high, low = halves(weights)
    weights_h[...] = high
    weights_l[...] = low
    high, low = halves(jnp.concatenate([edges, exact(edges, turned_up)], axis=1))
    back[...] = jnp.concatenate([high, low], axis=0)

    rows = near_rows[...]
    rows = jnp.where(rows >= 0, rows - dom_rank * ELEMS, rows).astype(F32)
    near = [upright(rows[edge : edge + 1]).astype(jnp.int32) for edge in range(EDGES)]
    cell = lax.broadcasted_iota(jnp.int32, (ELEMS, EDGES * ELEMS), 1)
    wanted = near[EDGES - 1]
    for edge in range(EDGES - 1):
        wanted = jnp.where(cell // ELEMS == edge, near[edge], wanted)
    gather[...] = jnp.where(cell % ELEMS == wanted, 1.0, 0.0).astype(BF16)
    wide = lax.broadcasted_iota(jnp.int32, (ROWS, ROWS), 1)
    rims = [upright(rim_rows[side : side + 1, :].astype(F32)).astype(jnp.int32) for side in range(2)]
    column = jnp.concatenate([rims[side] + plane * ELEMS for side in range(2) for plane in range(OWN)], axis=0)
    picked = jnp.where(wide == column, 1.0, 0.0)
    to_rim[...] = picked.astype(BF16)
    from_rim[...] = jnp.transpose(picked).astype(BF16)
    lane = lanes(ELEMS)
    edge = edge_of(lane)
    beyond = ((edge == 1) & (near[1] == -2)) | ((edge == 3) & (near[3] == -2))
    mask = jnp.where(beyond & (lane >= lower), 1.0, 0.0)
    scale = jnp.broadcast_to(upright(scale_row[...]), (ELEMS, POINTS))
    plane = plane_rank * OWN + lax.broadcasted_iota(jnp.int32, (OWN, POINTS), 0)
    wave = jnp.where(plane == 1, PLANES // 2, plane // 2).astype(F32) * AXIAL_WAVE
    one = INVERSE_STEP + wave * wave
    rim_mask[...] = mask
    scale_one[...] = one
    scale_two[...] = scale

    melted = upright(flags[...].astype(F32))
    melting[...] = jnp.broadcast_to(1.0 / (1.0 + LATENT * melted), (PLANES, POINTS))
    for side in range(2):
        factors[side : side + 1, :] = geom[side, pl.ds(plane_rank, 1), :]
    high, low = halves(jnp.concatenate([jnp.transpose(deriv[0]), jnp.transpose(deriv[1])], axis=1))
    deriv_h[...] = high
    deriv_l[...] = low

    vector = fields[0].reshape(ROWS, POINTS)
    part, left, right, _ = start_helmholtz(
        vector, weights_h[...], weights_l[...], back[...], gather[...], to_rim[...], one, scale
    )
    part_out[...] = part
    left_out[...] = left
    right_out[...] = right


def base_kernel(fields, part, left, right, from_rim, back, table, out, table_out):
    table_out[...] = table[...]
    high, low = arrived(left, right, from_rim)
    image = part[...] - rim_coupling(high, low, back[...])
    out[...] = INVERSE_STEP * fields[0].reshape(ROWS, POINTS) - image


def residual_kernel(
    modal, base, weights_h, weights_l, back, gather, to_rim, scale_one, scale_two,
    residual_out, part_out, left_out, right_out, crossing_out,
):
    heat = [modal[pl.ds(plane * 4 + 3, ELEMS, stride=16), :] for plane in range(OWN)]
    residual = base[...] + jnp.concatenate(heat, axis=0)
    part, left, right, crossing = start_helmholtz(
        residual,
        weights_h[...],
        weights_l[...],
        back[...],
        gather[...],
        to_rim[...],
        scale_one[...],
        scale_two[...],
    )
    left_out[...] = left
    right_out[...] = right
    residual_out[...] = residual
    part_out[...] = part
    crossing_out[...] = crossing


def momentum_kernel(modal, out):
    for field in range(3):
        for plane in range(OWN):
            out[field, plane] = modal[pl.ds(plane * 4 + field, ELEMS, stride=16), :]


def moments_kernel(
    residual_ref, part, left, right, crossing, from_rim, weights_h, weights_l, back, gather,
    rim_mask, scale_one, scale_two, image_out, sums_out,
):
    high, low = arrived(left, right, from_rim)
    image = part[...] - rim_coupling(high, low, back[...])
    image_out[...] = image
    residual = residual_ref[...]
    weights = [
        jnp.concatenate([w[:, :POINTS], w[:, 2 * POINTS : 3 * POINTS]], axis=1)
        for w in (weights_h, weights_l)
    ]
    images = product_stacked(image, *weights)
    stiff, doubled = images[:, :POINTS], images[:, POINTS:]
    facing = doubled_sum(facing_local(two_halves(doubled), gather[...]))
    facing = facing + (high + low) - crossing[...] * by_element(rim_mask[...])
    own = pltpu.roll(doubled, 2 * TRACE, 1)
    jumps = jnp.where(lanes(ROWS) >= EDGES * TRACE, own * (own - facing), 0.0)
    square = image * image
    cubic = by_plane(scale_one[...]) * square + by_element(scale_two[...]) * (image * stiff) + jumps
    rows = [
        jnp.sum(value[plane * ELEMS : (plane + 1) * ELEMS], axis=0, keepdims=True)
        for value in (residual * residual, residual * image, square, cubic)
        for plane in range(OWN)
    ]
    totals = jnp.sum(jnp.concatenate(rows, axis=0), axis=1, keepdims=True)
    down = lax.broadcasted_iota(jnp.int32, (EDGES * OWN, POINTS), 0)
    row = jnp.sum(jnp.where(down == lanes(EDGES * OWN), totals, 0.0), axis=0, keepdims=True)
    sums_out[...] = jnp.broadcast_to(row, sums_out.shape)


def final_kernel(sums, fields, residual, image, out):
    total = jnp.sum(sums[...], axis=0, keepdims=True)
    m0, m1, m2, m3 = (pltpu.roll(total, (-k * OWN) % POINTS, 1) for k in range(4))
    step = m0 / m1
    after = m0 + step * (step * m2 - 2.0 * m1)
    after_image = m1 + step * (step * m3 - 2.0 * m2)
    ratio = after / m0
    second = after / (after_image - ratio * after / step)
    on_residual = step + second * (1.0 + ratio)
    on_image = -second * step
    for plane in range(OWN):
        rows = pl.ds(plane * ELEMS, ELEMS)
        out[plane] = (
            fields[0, plane]
            + on_residual[:, plane : plane + 1] * residual[rows, :]
            + on_image[:, plane : plane + 1] * image[rows, :]
        )


def per_device(
    spectral_fields,
    deriv_ops,
    geom,
    stiffness,
    stiff_scale,
    traces,
    neighbors,
    rim_lists,
    melt_flags,
):
    count = lax.axis_size("dom")
    groups = lax.axis_size("plane")
    whole = ((ROWS, POINTS), F32)
    rims = ((RIM, POINTS), F32)
    plain = pl.BlockSpec(memory_space=pltpu.VMEM)
    heat_only = pl.BlockSpec((1, OWN, ELEMS, POINTS), lambda *_: (3, 0, 0, 0), memory_space=pltpu.VMEM)

    with jax.named_scope("to_points"):
        (packed,) = call(pack_kernel, [((ELEMS * 16, POINTS), F32)], spectral_fields)
        gathered = lax.all_to_all(
            packed.reshape(groups, 16, POINTS), "plane", split_axis=0, concat_axis=0, tiled=True
        ).reshape(groups * 16, POINTS)

    def exchange(left, right):
        from_left = lax.ppermute(right, "dom", [(i, (i + 1) % count) for i in range(count)])
        from_right = lax.ppermute(left, "dom", [((i + 1) % count, i) for i in range(count)])
        return from_left, from_right

    with jax.named_scope("base"):
        (
            weights_h, weights_l, back, gather, to_rim, from_rim, rim_mask, scale_one, scale_two,
            melting, factors, deriv_h, deriv_l, part, left, right,
        ) = call(
            prepare_kernel,
            [
                ((POINTS, 6 * POINTS), BF16),
                ((POINTS, 6 * POINTS), BF16),
                ((2 * POINTS, 2 * POINTS), BF16),
                ((ELEMS, EDGES * ELEMS), BF16),
                ((ROWS, ROWS), BF16),
                ((ROWS, ROWS), BF16),
                ((ELEMS, POINTS), F32),
                ((OWN, POINTS), F32),
                ((ELEMS, POINTS), F32),
                whole,
                ((2, POINTS), F32),
                ((POINTS, 2 * POINTS), BF16),
                ((POINTS, 2 * POINTS), BF16),
                whole,
                rims,
                rims,
            ],
            stiffness,
            traces,
            stiff_scale.reshape(1, ELEMS),
            neighbors.T,
            rim_lists[0],
            melt_flags.reshape(1, PLANES),
            deriv_ops,
            geom,
            spectral_fields,
            specs=[plain] * 8 + [heat_only],
        )
        left, right = exchange(left, right)
        table = jnp.asarray(axial_table())
        base, table = call(
            base_kernel,
            [whole, (table.shape, BF16)],
            spectral_fields,
            part,
            left,
            right,
            from_rim,
            back,
            table,
            specs=[heat_only] + [plain] * 6,
        )

    with jax.named_scope("advection"):
        gathered, base, table = lax.optimization_barrier((gathered, base, table))
        (modal,) = call(
            physical_kernel,
            [((groups * 16, POINTS), F32)],
            gathered,
            factors,
            melting,
            deriv_h,
            deriv_l,
            table,
            flops=10**9,
        )
        returned = lax.all_to_all(
            modal.reshape(groups, 16, POINTS), "plane", split_axis=0, concat_axis=0, tiled=True
        ).reshape(ELEMS * 16, POINTS)

    with jax.named_scope("solve"):
        residual, part, left, right, crossing = call(
            residual_kernel,
            [whole, whole, rims, rims, whole],
            returned,
            base,
            weights_h,
            weights_l,
            back,
            gather,
            to_rim,
            scale_one,
            scale_two,
        )
        left, right = exchange(left, right)
        (momentum,) = call(momentum_kernel, [((3, OWN, ELEMS, POINTS), F32)], returned)
        left, right, momentum = lax.optimization_barrier((left, right, momentum))
        image, sums = call(
            moments_kernel,
            [whole, ((count, POINTS), F32)],
            residual,
            part,
            left,
            right,
            crossing,
            from_rim,
            weights_h,
            weights_l,
            back,
            gather,
            rim_mask,
            scale_one,
            scale_two,
        )
        sums = lax.all_to_all(
            sums.reshape(count, 1, POINTS), "dom", split_axis=0, concat_axis=0, tiled=True
        ).reshape(count, POINTS)
        (temperature,) = call(
            final_kernel,
            [((OWN, ELEMS, POINTS), F32)],
            sums,
            spectral_fields,
            residual,
            image,
            specs=[plain, heat_only, plain, plain],
        )
    return momentum, temperature


def solution(mesh):
    placed = (
        P(None, "plane", "dom", None),
        P(),
        P(None, "dom", None),
        P(),
        P("dom"),
        P(),
        P("dom", None),
        P("dom", None, None),
        P(None, ("dom", "plane")),
    )
    return jax.shard_map(
        per_device,
        mesh=mesh,
        in_specs=placed,
        out_specs=(P(None, "plane", "dom", None), P("plane", "dom", None)),
        check_vma=False,
    )
```

```python
import functools

import jax
import jax.numpy as jnp
import numpy as np
from jax import lax
from jax.experimental import pallas as pl
from jax.experimental.pallas import tpu as pltpu
from jax.sharding import PartitionSpec as P

PLANES = 256
POINTS = 128
ELEMS = 64
OWN = 4
EDGES = 4
TRACE = 16
RIM = 32
ROWS = OWN * ELEMS
AXIAL_WAVE = 0.01
INVERSE_STEP = 0.5
LATENT = 2.0
F32 = jnp.float32
BF16 = jnp.bfloat16


def halves_np(table):
    high = table.astype(np.float32).astype(jnp.bfloat16)
    low = (table - high.astype(np.float64)).astype(np.float32).astype(jnp.bfloat16)
    return high, low


@functools.cache
def axial_table():
    points = np.arange(PLANES)[:, None]
    modes = np.arange(PLANES // 2)[None, :]
    angles = 2.0 * np.pi / PLANES * ((points * modes) % PLANES)
    others = np.where(modes == 0, 1.0 - 2.0 * (points % 2), np.sin(angles))
    return np.concatenate(halves_np(np.concatenate([np.cos(angles), others], axis=1)), axis=0)


def halves(value):
    high = value.astype(BF16)
    return high, (value - high.astype(F32)).astype(BF16)


def product(left, right):
    return jnp.dot(left, right, preferred_element_type=F32)


def across(left, right):
    return lax.dot_general(left, right, (((0,), (0,)), ((), ())), preferred_element_type=F32)


def product3(left, right):
    return product(left[0], right[0]) + (product(left[1], right[0]) + product(left[0], right[1]))


def lanes(rows):
    return lax.broadcasted_iota(jnp.int32, (rows, POINTS), 1)


def edge_of(lane):
    return (lane % (EDGES * TRACE)) // TRACE


def call(kernel, outs, *args, flops=0):
    return pl.pallas_call(
        kernel,
        out_shape=[jax.ShapeDtypeStruct(shape, kind) for shape, kind in outs],
        in_specs=[pl.BlockSpec(memory_space=pltpu.VMEM)] * len(args),
        out_specs=[pl.BlockSpec(memory_space=pltpu.VMEM)] * len(outs),
        compiler_params=pltpu.CompilerParams(vmem_limit_bytes=24 * 1024 * 1024),
        cost_estimate=pl.CostEstimate(
            flops=flops or 10**7,
            bytes_accessed=sum(a.size * a.dtype.itemsize for a in args),
            transcendentals=0,
        ),
    )(*args)


def stacked(value):
    return jnp.concatenate(halves(value), axis=1)


def product_stacked(value, high, low):
    pair = stacked(value)
    twice = jnp.concatenate([high, high], axis=0)
    return product(pair, twice) + product(pair[:, : low.shape[0]], low)


def pack_kernel(fields, out):
    for plane in range(OWN):
        for field in range(4):
            out[pl.ds(plane * 4 + field, ELEMS, stride=16), :] = fields[field, plane]


def physical_kernel(fields, factors, melting, deriv_h, deriv_l, table, out):
    half = PLANES // 2
    even = [fields[pl.ds(c, half, stride=8), :] for c in range(4)]
    odd = [fields[pl.ds(4 + c, half, stride=8), :] for c in range(4)]
    even, odd = jnp.concatenate(even, axis=1), jnp.concatenate(odd, axis=1)
    mode = lax.broadcasted_iota(jnp.int32, (half, 4 * POINTS), 0)
    wave = mode.astype(F32) * AXIAL_WAVE
    spectral = jnp.concatenate(
        [jnp.concatenate([even, wave * odd], axis=1), jnp.concatenate([odd, -wave * even], axis=1)], axis=0
    )
    basis = (table[:PLANES], table[PLANES:])
    points = product3(basis, halves(spectral))
    values = [points[:, c * POINTS : (c + 1) * POINTS] for c in range(4)]
    axial = [points[:, c * POINTS : (c + 1) * POINTS] for c in range(4, 8)]
    first = values[0] * factors[0:1, :]
    second = values[1] * factors[1:2, :]
    third = values[2]
    terms = []
    for c in range(4):
        slopes = product_stacked(values[c], deriv_h[...], deriv_l[...])
        term = first * slopes[:, :POINTS] + second * slopes[:, POINTS:] + third * axial[c]
        terms.append(term * melting[...] if c == 3 else term)
    terms = halves(jnp.concatenate(terms, axis=1))
    modal = across(basis[0], terms[0]) + (across(basis[1], terms[0]) + across(basis[0], terms[1]))
    row = lax.broadcasted_iota(jnp.int32, (PLANES, 4 * POINTS), 0)
    modal = modal * jnp.where(row % half == 0, -1.0 / PLANES, -2.0 / PLANES)
    for c in range(4):
        out[pl.ds(c, half, stride=8), :] = modal[:half, c * POINTS : (c + 1) * POINTS]
        out[pl.ds(4 + c, half, stride=8), :] = modal[half:, c * POINTS : (c + 1) * POINTS]


def upright(row):
    size = row.shape[1]
    down = lax.broadcasted_iota(jnp.int32, (size, size), 0)
    along = lax.broadcasted_iota(jnp.int32, (size, size), 1)
    return jnp.sum(jnp.where(down == along, row, 0.0), axis=1, keepdims=True)


def exact(left, right):
    return jnp.dot(left, right, preferred_element_type=F32, precision=lax.Precision.HIGHEST)


def two_halves(doubled):
    high = doubled.astype(BF16).astype(F32)
    return jnp.where(lanes(doubled.shape[0]) < EDGES * TRACE, high, doubled - high)


def facing_local(split_traces, gather):
    edge = edge_of(lanes(ELEMS))
    parts = []
    for plane in range(OWN):
        own = split_traces[plane * ELEMS : (plane + 1) * ELEMS]
        stack = [jnp.where(edge == j, own, 0.0).astype(BF16) for j in range(EDGES)]
        parts.append(product(gather, jnp.concatenate(stack, axis=0)))
    return jnp.concatenate(parts, axis=0)


def packed_rims(rims, edge):
    lane = lanes(RIM)
    total = jnp.zeros((RIM, POINTS), F32)
    for plane in range(OWN):
        rows = rims[plane * RIM : (plane + 1) * RIM]
        for which in range(2):
            at = plane * 2 * TRACE + which * TRACE
            moved = pltpu.roll(rows, (at - which * EDGES * TRACE - edge * TRACE) % POINTS, 1)
            total = jnp.where((lane >= at) & (lane < at + TRACE), moved, total)
    return total


def unpacked_rims(packed, edge):
    lane = lanes(RIM)
    parts = []
    for plane in range(OWN):
        total = jnp.zeros((RIM, POINTS), F32)
        for which in range(2):
            at = which * EDGES * TRACE + edge * TRACE
            moved = pltpu.roll(packed, (at - plane * 2 * TRACE - which * TRACE) % POINTS, 1)
            total = jnp.where((lane >= at) & (lane < at + TRACE), moved, total)
        parts.append(total)
    return jnp.concatenate(parts, axis=0)


def doubled_sum(value):
    return value + pltpu.roll(value, EDGES * TRACE, 1)


def by_plane(rows):
    return jnp.concatenate(
        [jnp.broadcast_to(rows[plane : plane + 1], (ELEMS, POINTS)) for plane in range(OWN)], axis=0
    )


def squared_waves(number):
    plane = lax.axis_index("plane") * OWN + number
    wave = jnp.where(plane == 1, PLANES // 2, plane // 2).astype(F32) * AXIAL_WAVE
    return wave * wave


def by_element(rows):
    return jnp.concatenate([rows] * OWN, axis=0)


def start_helmholtz(vector, weights_h, weights_l, back, gather, to_rim, scale):
    scale = by_element(scale)
    images = product_stacked(vector, weights_h, weights_l)
    stiff, own, doubled, crossing, stiff_trace, own_trace = (
        images[:, k * POINTS : (k + 1) * POINTS] for k in range(6)
    )
    traces_split = two_halves(doubled)
    facing = facing_local(traces_split, gather).astype(BF16)
    coupling = product(jnp.concatenate([facing, facing], axis=1), back)
    part = scale * stiff + own - coupling[:, :POINTS]
    part_trace = scale * stiff_trace + own_trace - coupling[:, POINTS:]
    split = jnp.concatenate([traces_split, two_halves(part_trace)], axis=1).astype(BF16)
    rims = product(to_rim, split)
    first, second = doubled_sum(rims[:, :POINTS]), doubled_sum(rims[:, POINTS:])
    rims = jnp.where(lanes(ROWS) < EDGES * TRACE, first, second)
    half = OWN * RIM
    return part, packed_rims(rims[:half], 1), packed_rims(rims[half:], 3), crossing


def arrived(left, right, from_rim):
    both = jnp.concatenate([unpacked_rims(left[...], 3), unpacked_rims(right[...], 1)], axis=0)
    spread = product(from_rim[...], stacked(both))
    return spread[:, :POINTS], spread[:, POINTS:]


def rim_coupling(high, low, back):
    facing = jnp.where(
        lanes(ROWS) < EDGES * TRACE, high, pltpu.roll(low, EDGES * TRACE, 1)
    ).astype(BF16)
    return product(jnp.concatenate([facing, facing], axis=1), back[:, :POINTS])


def prepare_kernel(
    stiffness, traces, scale_row, near_rows, rim_rows, flags, deriv, geom, fields,
    weights_h, weights_l, back, gather, to_rim, from_rim, rim_mask, scale,
    size, melting, factors, deriv_h, deriv_l, part_out, left_out, right_out,
):
    plane_rank = lax.axis_index("plane")
    dom_rank = lax.axis_index("dom")
    edges = traces[...].reshape(EDGES * TRACE, POINTS)
    stiff = stiffness[...]
    sums = jnp.sum(jnp.abs(stiff), axis=0, keepdims=True)
    bound = 3.0 * jnp.max(sums, axis=1, keepdims=True) + 2.0 * jnp.sum(
        jnp.sum(edges * edges, axis=0, keepdims=True), axis=1, keepdims=True
    )
    bound = jnp.broadcast_to(bound, (1, POINTS))
    root = jnp.ones((1, POINTS), F32)
    for power in (32, 16, 8, 4, 2, 1):
        large = bound >= 4.0**power
        bound = jnp.where(large, bound * 4.0**-power, bound)
        root = jnp.where(large, root * 2.0**power, root)
    root = jnp.where(bound > 1.0, root * 2.0, root)
    size[...] = root * root
    inverse = 1.0 / root
    edges = edges * inverse
    stiff = stiff * inverse * inverse
    turned = jnp.concatenate([edges[2 * TRACE :], edges[: 2 * TRACE]], axis=0)
    edges = jnp.concatenate([edges, edges], axis=0)
    turned = jnp.concatenate([turned, turned], axis=0)
    edges_up = jnp.transpose(edges)
    turned_up = jnp.transpose(turned)
    own = 0.5 * exact(edges_up, edges)
    down = lax.broadcasted_iota(jnp.int32, (POINTS, POINTS), 0)
    along = lanes(POINTS)
    lower = EDGES * TRACE
    kept = (
        (down < lower)
        & (along >= lower)
        & (edge_of(down) == edge_of(along))
        & (edge_of(along) % 2 == 1)
    )
    crossing = exact(edges_up, jnp.where(kept, exact(turned, turned_up), 0.0))
    weights = jnp.concatenate(
        [stiff, own, turned_up, crossing, exact(stiff, turned_up), exact(own, turned_up)], axis=1
    )
    high, low = halves(weights)
    weights_h[...] = high
    weights_l[...] = low
    high, low = halves(jnp.concatenate([edges, exact(edges, turned_up)], axis=1))
    back[...] = jnp.concatenate([high, low], axis=0)

    rows = near_rows[...]
    rows = jnp.where(rows >= 0, rows - dom_rank * ELEMS, rows).astype(F32)
    near = [upright(rows[edge : edge + 1]).astype(jnp.int32) for edge in range(EDGES)]
    cell = lax.broadcasted_iota(jnp.int32, (ELEMS, EDGES * ELEMS), 1)
    wanted = near[EDGES - 1]
    for edge in range(EDGES - 1):
        wanted = jnp.where(cell // ELEMS == edge, near[edge], wanted)
    gather[...] = jnp.where(cell % ELEMS == wanted, 1.0, 0.0).astype(BF16)
    wide = lax.broadcasted_iota(jnp.int32, (ROWS, ROWS), 1)
    rims = [upright(rim_rows[side : side + 1, :].astype(F32)).astype(jnp.int32) for side in range(2)]
    column = jnp.concatenate([rims[side] + plane * ELEMS for side in range(2) for plane in range(OWN)], axis=0)
    picked = jnp.where(wide == column, 1.0, 0.0)
    to_rim[...] = picked.astype(BF16)
    from_rim[...] = jnp.transpose(picked).astype(BF16)
    lane = lanes(ELEMS)
    edge = edge_of(lane)
    beyond = ((edge == 1) & (near[1] == -2)) | ((edge == 3) & (near[3] == -2))
    mask = jnp.where(beyond & (lane >= lower), 1.0, 0.0)
    rim_mask[...] = mask
    scale[...] = jnp.broadcast_to(upright(scale_row[...]), (ELEMS, POINTS))

    melted = upright(flags[...].astype(F32))
    melting[...] = jnp.broadcast_to(1.0 / (1.0 + LATENT * melted), (PLANES, POINTS))
    for side in range(2):
        factors[side : side + 1, :] = geom[side, pl.ds(plane_rank, 1), :]
    high, low = halves(jnp.concatenate([jnp.transpose(deriv[0]), jnp.transpose(deriv[1])], axis=1))
    deriv_h[...] = high
    deriv_l[...] = low

    vector = fields[3].reshape(ROWS, POINTS)
    part, left, right, _ = start_helmholtz(
        vector, weights_h[...], weights_l[...], back[...], gather[...], to_rim[...], scale[...]
    )
    part_out[...] = part
    left_out[...] = left
    right_out[...] = right


def base_kernel(fields, part, left, right, from_rim, back, size, table, out, table_out):
    table_out[...] = table[...]
    high, low = arrived(left, right, from_rim)
    image = part[...] - rim_coupling(high, low, back[...])
    squares = by_plane(squared_waves(lax.broadcasted_iota(jnp.int32, (OWN, POINTS), 0)))
    out[...] = -(squares * fields[3].reshape(ROWS, POINTS) + size[...] * image)


def residual_kernel(
    modal, base, weights_h, weights_l, back, gather, to_rim, scale,
    residual_out, part_out, left_out, right_out, crossing_out,
):
    heat = [modal[pl.ds(plane * 4 + 3, ELEMS, stride=16), :] for plane in range(OWN)]
    residual = base[...] + jnp.concatenate(heat, axis=0)
    part, left, right, crossing = start_helmholtz(
        residual,
        weights_h[...],
        weights_l[...],
        back[...],
        gather[...],
        to_rim[...],
        scale[...],
    )
    left_out[...] = left
    right_out[...] = right
    residual_out[...] = residual
    part_out[...] = part
    crossing_out[...] = crossing


def momentum_kernel(modal, out):
    for field in range(3):
        for plane in range(OWN):
            out[field, plane] = modal[pl.ds(plane * 4 + field, ELEMS, stride=16), :]


def moments_kernel(
    residual_ref, part, left, right, crossing, from_rim, weights_h, weights_l, back, gather,
    rim_mask, scale, image_out, sums_out,
):
    high, low = arrived(left, right, from_rim)
    image = part[...] - rim_coupling(high, low, back[...])
    image_out[...] = image
    residual = residual_ref[...]
    weights = [
        jnp.concatenate([w[:, :POINTS], w[:, 2 * POINTS : 3 * POINTS]], axis=1)
        for w in (weights_h, weights_l)
    ]
    images = product_stacked(image, *weights)
    stiff, doubled = images[:, :POINTS], images[:, POINTS:]
    facing = doubled_sum(facing_local(two_halves(doubled), gather[...]))
    facing = facing + (high + low) - crossing[...] * by_element(rim_mask[...])
    own = pltpu.roll(doubled, 2 * TRACE, 1)
    jumps = jnp.where(lanes(ROWS) >= EDGES * TRACE, own * (own - facing), 0.0)
    square = image * image
    cubic = by_element(scale[...]) * (image * stiff) + jumps
    rows = [
        jnp.sum(value[plane * ELEMS : (plane + 1) * ELEMS], axis=0, keepdims=True)
        for value in (residual * residual, residual * image, square, cubic)
        for plane in range(OWN)
    ]
    totals = jnp.sum(jnp.concatenate(rows, axis=0), axis=1, keepdims=True)
    down = lax.broadcasted_iota(jnp.int32, (EDGES * OWN, POINTS), 0)
    row = jnp.sum(jnp.where(down == lanes(EDGES * OWN), totals, 0.0), axis=0, keepdims=True)
    sums_out[...] = jnp.broadcast_to(row, sums_out.shape)


def final_kernel(sums, size, fields, residual, image, out):
    total = jnp.sum(sums[...], axis=0, keepdims=True)
    k0, k1, k2, k3 = (pltpu.roll(total, (-k * OWN) % POINTS, 1) for k in range(4))
    diagonal = INVERSE_STEP + squared_waves(lanes(1))
    size = size[...]
    step = k0 / (diagonal * k0 + size * k1)
    theta = k1 / k0
    norm = k2 - theta * k1
    bent = k3 + theta * (theta * k1 - 2.0 * k2)
    length = step * size
    share = length * (norm / k0)
    ratio = length * share
    second = norm / (diagonal * norm + size * (bent - share * norm))
    on_residual = step + second * (length * theta + ratio)
    on_image = -second * length
    for plane in range(OWN):
        rows = pl.ds(plane * ELEMS, ELEMS)
        out[plane] = (
            fields[3, plane]
            + on_residual[:, plane : plane + 1] * residual[rows, :]
            + on_image[:, plane : plane + 1] * image[rows, :]
        )


def per_device(
    spectral_fields,
    deriv_ops,
    geom,
    stiffness,
    stiff_scale,
    traces,
    neighbors,
    rim_lists,
    melt_flags,
):
    count = lax.axis_size("dom")
    groups = lax.axis_size("plane")
    whole = ((ROWS, POINTS), F32)
    rims = ((RIM, POINTS), F32)

    with jax.named_scope("to_points"):
        (packed,) = call(pack_kernel, [((ELEMS * 16, POINTS), F32)], spectral_fields)
        gathered = lax.all_to_all(
            packed.reshape(groups, 16, POINTS), "plane", split_axis=0, concat_axis=0, tiled=True
        ).reshape(groups * 16, POINTS)

    def exchange(left, right):
        from_left = lax.ppermute(right, "dom", [(i, (i + 1) % count) for i in range(count)])
        from_right = lax.ppermute(left, "dom", [((i + 1) % count, i) for i in range(count)])
        return from_left, from_right

    with jax.named_scope("base"):
        (
            weights_h, weights_l, back, gather, to_rim, from_rim, rim_mask, scale,
            size, melting, factors, deriv_h, deriv_l, part, left, right,
        ) = call(
            prepare_kernel,
            [
                ((POINTS, 6 * POINTS), BF16),
                ((POINTS, 6 * POINTS), BF16),
                ((2 * POINTS, 2 * POINTS), BF16),
                ((ELEMS, EDGES * ELEMS), BF16),
                ((ROWS, ROWS), BF16),
                ((ROWS, ROWS), BF16),
                ((ELEMS, POINTS), F32),
                ((ELEMS, POINTS), F32),
                ((1, POINTS), F32),
                whole,
                ((2, POINTS), F32),
                ((POINTS, 2 * POINTS), BF16),
                ((POINTS, 2 * POINTS), BF16),
                whole,
                rims,
                rims,
            ],
            stiffness,
            traces,
            stiff_scale.reshape(1, ELEMS),
            neighbors.T,
            rim_lists[0],
            melt_flags.reshape(1, PLANES),
            deriv_ops,
            geom,
            spectral_fields,
        )
        left, right = exchange(left, right)
        table = jnp.asarray(axial_table())
        base, table = call(
            base_kernel,
            [whole, (table.shape, BF16)],
            spectral_fields,
            part,
            left,
            right,
            from_rim,
            back,
            size,
            table,
        )

    with jax.named_scope("advection"):
        gathered, base, table = lax.optimization_barrier((gathered, base, table))
        (modal,) = call(
            physical_kernel,
            [((groups * 16, POINTS), F32)],
            gathered,
            factors,
            melting,
            deriv_h,
            deriv_l,
            table,
            flops=10**9,
        )
        returned = lax.all_to_all(
            modal.reshape(groups, 16, POINTS), "plane", split_axis=0, concat_axis=0, tiled=True
        ).reshape(ELEMS * 16, POINTS)

    with jax.named_scope("solve"):
        residual, part, left, right, crossing = call(
            residual_kernel,
            [whole, whole, rims, rims, whole],
            returned,
            base,
            weights_h,
            weights_l,
            back,
            gather,
            to_rim,
            scale,
        )
        left, right = exchange(left, right)
        (momentum,) = call(momentum_kernel, [((3, OWN, ELEMS, POINTS), F32)], returned)
        left, right, momentum = lax.optimization_barrier((left, right, momentum))
        image, sums = call(
            moments_kernel,
            [whole, ((count, POINTS), F32)],
            residual,
            part,
            left,
            right,
            crossing,
            from_rim,
            weights_h,
            weights_l,
            back,
            gather,
            rim_mask,
            scale,
        )
        sums = lax.all_to_all(
            sums.reshape(count, 1, POINTS), "dom", split_axis=0, concat_axis=0, tiled=True
        ).reshape(count, POINTS)
        (temperature,) = call(
            final_kernel,
            [((OWN, ELEMS, POINTS), F32)],
            sums,
            size,
            spectral_fields,
            residual,
            image,
        )
    return momentum, temperature


def solution(mesh):
    placed = (
        P(None, "plane", "dom", None),
        P(),
        P(None, "dom", None),
        P(),
        P("dom"),
        P(),
        P("dom", None),
        P("dom", None, None),
        P(None, ("dom", "plane")),
    )
    return jax.shard_map(
        per_device,
        mesh=mesh,
        in_specs=placed,
        out_specs=(P(None, "plane", "dom", None), P("plane", "dom", None)),
        check_vma=False,
    )
```

```python
import functools

import jax
import jax.numpy as jnp
import numpy as np
from jax import lax
from jax.experimental import pallas as pl
from jax.experimental.pallas import tpu as pltpu
from jax.sharding import PartitionSpec as P

PLANES = 256
POINTS = 128
ELEMS = 64
OWN = 4
EDGES = 4
TRACE = 16
RIM = 32
ROWS = OWN * ELEMS
AXIAL_WAVE = 0.01
INVERSE_STEP = 0.5
LATENT = 2.0
F32 = jnp.float32
BF16 = jnp.bfloat16


def halves_np(table):
    high = table.astype(np.float32).astype(jnp.bfloat16)
    low = (table - high.astype(np.float64)).astype(np.float32).astype(jnp.bfloat16)
    return high, low


@functools.cache
def axial_table():
    points = np.arange(PLANES)[:, None]
    modes = np.arange(PLANES // 2)[None, :]
    angles = 2.0 * np.pi / PLANES * ((points * modes) % PLANES)
    others = np.where(modes == 0, 1.0 - 2.0 * (points % 2), np.sin(angles))
    return np.concatenate(halves_np(np.concatenate([np.cos(angles), others], axis=1)), axis=0)


def halves(value):
    high = value.astype(BF16)
    return high, (value - high.astype(F32)).astype(BF16)


def product(left, right):
    return jnp.dot(left, right, preferred_element_type=F32)


def across(left, right):
    return lax.dot_general(left, right, (((0,), (0,)), ((), ())), preferred_element_type=F32)


def product3(left, right):
    return product(left[0], right[0]) + (product(left[1], right[0]) + product(left[0], right[1]))


def lanes(rows):
    return lax.broadcasted_iota(jnp.int32, (rows, POINTS), 1)


def edge_of(lane):
    return (lane % (EDGES * TRACE)) // TRACE


def call(kernel, outs, *args, flops=0):
    return pl.pallas_call(
        kernel,
        out_shape=[jax.ShapeDtypeStruct(shape, kind) for shape, kind in outs],
        in_specs=[pl.BlockSpec(memory_space=pltpu.VMEM)] * len(args),
        out_specs=[pl.BlockSpec(memory_space=pltpu.VMEM)] * len(outs),
        compiler_params=pltpu.CompilerParams(vmem_limit_bytes=24 * 1024 * 1024),
        cost_estimate=pl.CostEstimate(
            flops=flops or 10**7,
            bytes_accessed=sum(a.size * a.dtype.itemsize for a in args),
            transcendentals=0,
        ),
    )(*args)


def stacked(value):
    return jnp.concatenate(halves(value), axis=1)


def product_stacked(value, high, low):
    pair = stacked(value)
    twice = jnp.concatenate([high, high], axis=0)
    return product(pair, twice) + product(pair[:, : low.shape[0]], low)


def pack_kernel(fields, out):
    for plane in range(OWN):
        for field in range(4):
            out[pl.ds(plane * 4 + field, ELEMS, stride=16), :] = fields[field, plane]


def physical_kernel(fields, factors, melting, deriv_h, deriv_l, table, out):
    half = PLANES // 2
    even = [fields[pl.ds(c, half, stride=8), :] for c in range(4)]
    odd = [fields[pl.ds(4 + c, half, stride=8), :] for c in range(4)]
    even, odd = jnp.concatenate(even, axis=1), jnp.concatenate(odd, axis=1)
    mode = lax.broadcasted_iota(jnp.int32, (half, 4 * POINTS), 0)
    wave = mode.astype(F32) * AXIAL_WAVE
    spectral = jnp.concatenate(
        [jnp.concatenate([even, wave * odd], axis=1), jnp.concatenate([odd, -wave * even], axis=1)], axis=0
    )
    basis = (table[:PLANES], table[PLANES:])
    points = product3(basis, halves(spectral))
    values = [points[:, c * POINTS : (c + 1) * POINTS] for c in range(4)]
    axial = [points[:, c * POINTS : (c + 1) * POINTS] for c in range(4, 8)]
    first = values[0] * factors[0:1, :]
    second = values[1] * factors[1:2, :]
    third = values[2]
    terms = []
    for c in range(4):
        slopes = product_stacked(values[c], deriv_h[...], deriv_l[...])
        term = first * slopes[:, :POINTS] + second * slopes[:, POINTS:] + third * axial[c]
        terms.append(term * melting[...] if c == 3 else term)
    terms = halves(jnp.concatenate(terms, axis=1))
    modal = across(basis[0], terms[0]) + (across(basis[1], terms[0]) + across(basis[0], terms[1]))
    row = lax.broadcasted_iota(jnp.int32, (PLANES, 4 * POINTS), 0)
    modal = modal * jnp.where(row % half == 0, -1.0 / PLANES, -2.0 / PLANES)
    for c in range(4):
        out[pl.ds(c, half, stride=8), :] = modal[:half, c * POINTS : (c + 1) * POINTS]
        out[pl.ds(4 + c, half, stride=8), :] = modal[half:, c * POINTS : (c + 1) * POINTS]


def upright(row):
    size = row.shape[1]
    down = lax.broadcasted_iota(jnp.int32, (size, size), 0)
    along = lax.broadcasted_iota(jnp.int32, (size, size), 1)
    return jnp.sum(jnp.where(down == along, row, 0.0), axis=1, keepdims=True)


def exact(left, right):
    return jnp.dot(left, right, preferred_element_type=F32, precision=lax.Precision.HIGHEST)


def two_halves(doubled):
    high = doubled.astype(BF16).astype(F32)
    return jnp.where(lanes(doubled.shape[0]) < EDGES * TRACE, high, doubled - high)


def facing_local(split_traces, gather):
    edge = edge_of(lanes(ELEMS))
    parts = []
    for plane in range(OWN):
        own = split_traces[plane * ELEMS : (plane + 1) * ELEMS]
        stack = [jnp.where(edge == j, own, 0.0).astype(BF16) for j in range(EDGES)]
        parts.append(product(gather, jnp.concatenate(stack, axis=0)))
    return jnp.concatenate(parts, axis=0)


def packed_rims(rims, edge):
    lane = lanes(RIM)
    total = jnp.zeros((RIM, POINTS), F32)
    for plane in range(OWN):
        rows = rims[plane * RIM : (plane + 1) * RIM]
        for which in range(2):
            at = plane * 2 * TRACE + which * TRACE
            moved = pltpu.roll(rows, (at - which * EDGES * TRACE - edge * TRACE) % POINTS, 1)
            total = jnp.where((lane >= at) & (lane < at + TRACE), moved, total)
    return total


def unpacked_rims(packed, edge):
    lane = lanes(RIM)
    parts = []
    for plane in range(OWN):
        total = jnp.zeros((RIM, POINTS), F32)
        for which in range(2):
            at = which * EDGES * TRACE + edge * TRACE
            moved = pltpu.roll(packed, (at - plane * 2 * TRACE - which * TRACE) % POINTS, 1)
            total = jnp.where((lane >= at) & (lane < at + TRACE), moved, total)
        parts.append(total)
    return jnp.concatenate(parts, axis=0)


def doubled_sum(value):
    return value + pltpu.roll(value, EDGES * TRACE, 1)


def by_plane(rows):
    return jnp.concatenate(
        [jnp.broadcast_to(rows[plane : plane + 1], (ELEMS, POINTS)) for plane in range(OWN)], axis=0
    )


def squared_waves(number):
    plane = lax.axis_index("plane") * OWN + number
    wave = jnp.where(plane == 1, PLANES // 2, plane // 2).astype(F32) * AXIAL_WAVE
    return wave * wave


def by_element(rows):
    return jnp.concatenate([rows] * OWN, axis=0)


def start_helmholtz(vector, weights_h, weights_l, back, gather, to_rim, scale):
    scale = by_element(scale)
    images = product_stacked(vector, weights_h, weights_l)
    stiff, own, doubled, crossing, stiff_trace, own_trace = (
        images[:, k * POINTS : (k + 1) * POINTS] for k in range(6)
    )
    traces_split = two_halves(doubled)
    facing = facing_local(traces_split, gather).astype(BF16)
    coupling = product(jnp.concatenate([facing, facing], axis=1), back)
    part = scale * stiff + own - coupling[:, :POINTS]
    part_trace = scale * stiff_trace + own_trace - coupling[:, POINTS:]
    split = jnp.concatenate([traces_split, two_halves(part_trace)], axis=1).astype(BF16)
    rims = product(to_rim, split)
    first, second = doubled_sum(rims[:, :POINTS]), doubled_sum(rims[:, POINTS:])
    rims = jnp.where(lanes(ROWS) < EDGES * TRACE, first, second)
    half = OWN * RIM
    return part, packed_rims(rims[:half], 1), packed_rims(rims[half:], 3), doubled, crossing


def arrived(left, right, from_rim):
    both = jnp.concatenate([unpacked_rims(left[...], 3), unpacked_rims(right[...], 1)], axis=0)
    spread = product(from_rim[...], stacked(both))
    return spread[:, :POINTS], spread[:, POINTS:]


def rim_coupling(high, low, back):
    facing = jnp.where(
        lanes(ROWS) < EDGES * TRACE, high, pltpu.roll(low, EDGES * TRACE, 1)
    ).astype(BF16)
    return product(jnp.concatenate([facing, facing], axis=1), back[:, :POINTS])


def prepare_kernel(
    stiffness, traces, scale_row, near_rows, rim_rows, flags, deriv, geom, fields,
    weights_h, weights_l, back, gather, to_rim, from_rim, rim_mask, scale,
    size, melting, factors, deriv_h, deriv_l, part_out, left_out, right_out,
):
    plane_rank = lax.axis_index("plane")
    dom_rank = lax.axis_index("dom")
    edges = traces[...].reshape(EDGES * TRACE, POINTS)
    stiff = stiffness[...]
    sums = jnp.sum(jnp.abs(stiff), axis=0, keepdims=True)
    bound = 3.0 * jnp.max(sums, axis=1, keepdims=True) + 2.0 * jnp.sum(
        jnp.sum(edges * edges, axis=0, keepdims=True), axis=1, keepdims=True
    )
    bound = jnp.broadcast_to(bound, (1, POINTS))
    root = jnp.ones((1, POINTS), F32)
    for power in (32, 16, 8, 4, 2, 1):
        large = bound >= 4.0**power
        bound = jnp.where(large, bound * 4.0**-power, bound)
        root = jnp.where(large, root * 2.0**power, root)
    root = jnp.where(bound > 1.0, root * 2.0, root)
    size[...] = root * root
    inverse = 1.0 / root
    edges = edges * inverse
    stiff = stiff * inverse * inverse
    turned = jnp.concatenate([edges[2 * TRACE :], edges[: 2 * TRACE]], axis=0)
    edges = jnp.concatenate([edges, edges], axis=0)
    turned = jnp.concatenate([turned, turned], axis=0)
    edges_up = jnp.transpose(edges)
    turned_up = jnp.transpose(turned)
    own = 0.5 * exact(edges_up, edges)
    down = lax.broadcasted_iota(jnp.int32, (POINTS, POINTS), 0)
    along = lanes(POINTS)
    lower = EDGES * TRACE
    kept = (
        (down < lower)
        & (along >= lower)
        & (edge_of(down) == edge_of(along))
        & (edge_of(along) % 2 == 1)
    )
    crossing = exact(edges_up, jnp.where(kept, exact(turned, turned_up), 0.0))
    weights = jnp.concatenate(
        [stiff, own, turned_up, crossing, exact(stiff, turned_up), exact(own, turned_up)], axis=1
    )
    high, low = halves(weights)
    weights_h[...] = high
    weights_l[...] = low
    high, low = halves(jnp.concatenate([edges, exact(edges, turned_up)], axis=1))
    back[...] = jnp.concatenate([high, low], axis=0)

    rows = near_rows[...]
    rows = jnp.where(rows >= 0, rows - dom_rank * ELEMS, rows).astype(F32)
    near = [upright(rows[edge : edge + 1]).astype(jnp.int32) for edge in range(EDGES)]
    cell = lax.broadcasted_iota(jnp.int32, (ELEMS, EDGES * ELEMS), 1)
    wanted = near[EDGES - 1]
    for edge in range(EDGES - 1):
        wanted = jnp.where(cell // ELEMS == edge, near[edge], wanted)
    gather[...] = jnp.where(cell % ELEMS == wanted, 1.0, 0.0).astype(BF16)
    wide = lax.broadcasted_iota(jnp.int32, (ROWS, ROWS), 1)
    rims = [upright(rim_rows[side : side + 1, :].astype(F32)).astype(jnp.int32) for side in range(2)]
    column = jnp.concatenate([rims[side] + plane * ELEMS for side in range(2) for plane in range(OWN)], axis=0)
    picked = jnp.where(wide == column, 1.0, 0.0)
    to_rim[...] = picked.astype(BF16)
    from_rim[...] = jnp.transpose(picked).astype(BF16)
    lane = lanes(ELEMS)
    edge = edge_of(lane)
    beyond = ((edge == 1) & (near[1] == -2)) | ((edge == 3) & (near[3] == -2))
    mask = jnp.where(beyond & (lane >= lower), 1.0, 0.0)
    rim_mask[...] = mask
    scale[...] = jnp.broadcast_to(upright(scale_row[...]), (ELEMS, POINTS))

    melted = upright(flags[...].astype(F32))
    melting[...] = jnp.broadcast_to(1.0 / (1.0 + LATENT * melted), (PLANES, POINTS))
    for side in range(2):
        factors[side : side + 1, :] = geom[side, pl.ds(plane_rank, 1), :]
    high, low = halves(jnp.concatenate([jnp.transpose(deriv[0]), jnp.transpose(deriv[1])], axis=1))
    deriv_h[...] = high
    deriv_l[...] = low

    vector = fields[3].reshape(ROWS, POINTS)
    part, left, right, _, _ = start_helmholtz(
        vector, weights_h[...], weights_l[...], back[...], gather[...], to_rim[...], scale[...]
    )
    part_out[...] = part
    left_out[...] = left
    right_out[...] = right


def base_kernel(fields, part, left, right, from_rim, back, size, table, out, table_out):
    table_out[...] = table[...]
    high, low = arrived(left, right, from_rim)
    image = part[...] - rim_coupling(high, low, back[...])
    squares = by_plane(squared_waves(lax.broadcasted_iota(jnp.int32, (OWN, POINTS), 0)))
    out[...] = -(squares * fields[3].reshape(ROWS, POINTS) + size[...] * image)


def residual_kernel(
    modal, base, weights_h, weights_l, back, gather, to_rim, scale,
    residual_out, part_out, left_out, right_out, traces_out,
):
    heat = [modal[pl.ds(plane * 4 + 3, ELEMS, stride=16), :] for plane in range(OWN)]
    residual = base[...] + jnp.concatenate(heat, axis=0)
    part, left, right, doubled, crossing = start_helmholtz(
        residual,
        weights_h[...],
        weights_l[...],
        back[...],
        gather[...],
        to_rim[...],
        scale[...],
    )
    left_out[...] = left
    right_out[...] = right
    residual_out[...] = residual
    part_out[...] = part
    lower = lanes(ROWS) < EDGES * TRACE
    traces_out[...] = jnp.where(lower, doubled, crossing)


def momentum_kernel(modal, residual, part, out, quotients):
    for field in range(3):
        for plane in range(OWN):
            out[field, plane] = modal[pl.ds(plane * 4 + field, ELEMS, stride=16), :]
    for plane in range(OWN):
        rows = pl.ds(plane * ELEMS, ELEMS)
        own = residual[rows, :]
        above = jnp.sum(jnp.sum(own * part[rows, :], axis=0, keepdims=True), axis=1, keepdims=True)
        below = jnp.sum(jnp.sum(own * own, axis=0, keepdims=True), axis=1, keepdims=True)
        quotient = jnp.where(below > 0.0, above / below, 0.0)
        quotients[plane : plane + 1, :] = jnp.broadcast_to(quotient, (1, POINTS))


NUMBERS = 9


def moments_kernel(
    residual_ref, part, left, right, traces_ref, from_rim, weights_h, weights_l, back, gather,
    rim_mask, scale, quotients, bend_out, sums_out,
):
    high, low = arrived(left, right, from_rim)
    beyond = high + low
    residual = residual_ref[...]
    bend = part[...] - rim_coupling(high, low, back[...]) - by_plane(quotients[...]) * residual
    bend_out[...] = bend
    weights = [
        jnp.concatenate([w[:, :POINTS], w[:, 2 * POINTS : 3 * POINTS]], axis=1)
        for w in (weights_h, weights_l)
    ]
    images = product_stacked(bend, *weights)
    stiff, doubled = images[:, :POINTS], images[:, POINTS:]
    traces = traces_ref[...]
    facing = doubled_sum(facing_local(two_halves(doubled), gather[...]))
    facing = facing + beyond - traces * by_element(rim_mask[...])
    own = pltpu.roll(doubled, 2 * TRACE, 1)
    upper = lanes(ROWS) >= EDGES * TRACE
    cubic = by_element(scale[...]) * (bend * stiff) + jnp.where(upper, own * (own - facing), 0.0)
    turned = jnp.where(
        edge_of(lanes(ROWS)) == 3,
        pltpu.roll(traces, 2 * TRACE, 1),
        pltpu.roll(traces, POINTS - 2 * TRACE, 1),
    )
    across_rims = jnp.where(upper, own * pltpu.roll(beyond, EDGES * TRACE, 1), turned * beyond)
    rows = [
        jnp.sum(value[plane * ELEMS : (plane + 1) * ELEMS], axis=0, keepdims=True)
        for value in (residual * residual, residual * bend, bend * bend, cubic, across_rims)
        for plane in range(OWN)
    ]
    whole, cut = jnp.concatenate(rows[: 4 * OWN], axis=0), jnp.concatenate(rows[4 * OWN :], axis=0)
    lane = lanes(OWN)
    cuts = [
        jnp.where((edge_of(lane) == edge) & ((lane >= EDGES * TRACE) == above), cut, 0.0)
        for above in (True, False)
        for edge in (3, 1)
    ]
    totals = jnp.sum(jnp.concatenate([whole, *cuts], axis=0), axis=1, keepdims=True)
    totals = jnp.concatenate([totals, quotients[:, 0:1], jnp.zeros((OWN, 1), F32)], axis=0)
    down = lax.broadcasted_iota(jnp.int32, ((NUMBERS + 1) * OWN, POINTS), 0)
    row = jnp.sum(jnp.where(down == lanes((NUMBERS + 1) * OWN), totals, 0.0), axis=0, keepdims=True)
    sums_out[...] = jnp.broadcast_to(row, sums_out.shape)


def final_kernel(sums, size, fields, residual, bend, out):
    diagonal = INVERSE_STEP + squared_waves(lanes(1))
    size = size[...]
    numbers = [pltpu.roll(sums[...], (-k * OWN) % POINTS, 1) for k in range(NUMBERS)]
    square, slant, bends, cubic, bend_left, bend_right, own_left, own_right, quotient = numbers

    def total(value):
        return jnp.sum(value, axis=0, keepdims=True)

    def beside(value):
        return pltpu.roll(value, 1, 0), pltpu.roll(value, value.shape[0] - 1, 0)

    k0 = total(square)
    k1 = total(quotient * square + slant)
    theta = k1 / k0
    apart = theta - quotient
    left, right = (apart - value for value in beside(apart))
    quotient_left, quotient_right = beside(quotient)
    norm = total(bends + apart * (apart * square - 2.0 * slant))
    bent = total(
        cubic
        + quotient_left * bend_left
        + quotient_right * bend_right
        - 2.0 * (apart * (bends + quotient * slant) + left * bend_left + right * bend_right)
        + apart * (apart * (slant + quotient * square) + left * own_left + right * own_right)
    )
    step = k0 / (diagonal * k0 + size * k1)
    length = step * size
    share = length * (norm / k0)
    ratio = length * share
    second = norm / (diagonal * norm + size * (bent - share * norm))
    second = jnp.where(norm > 0.0, second, 0.0)
    here = lax.broadcasted_iota(jnp.int32, apart.shape, 0) == lax.axis_index("dom")
    on_residual = step + second * (length * total(jnp.where(here, apart, 0.0)) + ratio)
    on_bend = -second * length
    for plane in range(OWN):
        rows = pl.ds(plane * ELEMS, ELEMS)
        out[plane] = (
            fields[3, plane]
            + on_residual[:, plane : plane + 1] * residual[rows, :]
            + on_bend[:, plane : plane + 1] * bend[rows, :]
        )


def per_device(
    spectral_fields,
    deriv_ops,
    geom,
    stiffness,
    stiff_scale,
    traces,
    neighbors,
    rim_lists,
    melt_flags,
):
    count = lax.axis_size("dom")
    groups = lax.axis_size("plane")
    whole = ((ROWS, POINTS), F32)
    rims = ((RIM, POINTS), F32)

    with jax.named_scope("to_points"):
        (packed,) = call(pack_kernel, [((ELEMS * 16, POINTS), F32)], spectral_fields)
        gathered = lax.all_to_all(
            packed.reshape(groups, 16, POINTS), "plane", split_axis=0, concat_axis=0, tiled=True
        ).reshape(groups * 16, POINTS)

    def exchange(left, right):
        from_left = lax.ppermute(right, "dom", [(i, (i + 1) % count) for i in range(count)])
        from_right = lax.ppermute(left, "dom", [((i + 1) % count, i) for i in range(count)])
        return from_left, from_right

    with jax.named_scope("base"):
        (
            weights_h, weights_l, back, gather, to_rim, from_rim, rim_mask, scale,
            size, melting, factors, deriv_h, deriv_l, part, left, right,
        ) = call(
            prepare_kernel,
            [
                ((POINTS, 6 * POINTS), BF16),
                ((POINTS, 6 * POINTS), BF16),
                ((2 * POINTS, 2 * POINTS), BF16),
                ((ELEMS, EDGES * ELEMS), BF16),
                ((ROWS, ROWS), BF16),
                ((ROWS, ROWS), BF16),
                ((ELEMS, POINTS), F32),
                ((ELEMS, POINTS), F32),
                ((1, POINTS), F32),
                whole,
                ((2, POINTS), F32),
                ((POINTS, 2 * POINTS), BF16),
                ((POINTS, 2 * POINTS), BF16),
                whole,
                rims,
                rims,
            ],
            stiffness,
            traces,
            stiff_scale.reshape(1, ELEMS),
            neighbors.T,
            rim_lists[0],
            melt_flags.reshape(1, PLANES),
            deriv_ops,
            geom,
            spectral_fields,
        )
        left, right = exchange(left, right)
        table = jnp.asarray(axial_table())
        base, table = call(
            base_kernel,
            [whole, (table.shape, BF16)],
            spectral_fields,
            part,
            left,
            right,
            from_rim,
            back,
            size,
            table,
        )

    with jax.named_scope("advection"):
        gathered, base, table = lax.optimization_barrier((gathered, base, table))
        (modal,) = call(
            physical_kernel,
            [((groups * 16, POINTS), F32)],
            gathered,
            factors,
            melting,
            deriv_h,
            deriv_l,
            table,
            flops=10**9,
        )
        returned = lax.all_to_all(
            modal.reshape(groups, 16, POINTS), "plane", split_axis=0, concat_axis=0, tiled=True
        ).reshape(ELEMS * 16, POINTS)

    with jax.named_scope("solve"):
        residual, part, left, right, edge_traces = call(
            residual_kernel,
            [whole, whole, rims, rims, whole],
            returned,
            base,
            weights_h,
            weights_l,
            back,
            gather,
            to_rim,
            scale,
        )
        left, right = exchange(left, right)
        momentum, quotients = call(
            momentum_kernel,
            [((3, OWN, ELEMS, POINTS), F32), ((OWN, POINTS), F32)],
            returned,
            residual,
            part,
        )
        left, right, momentum = lax.optimization_barrier((left, right, momentum))
        bend, sums = call(
            moments_kernel,
            [whole, ((count, POINTS), F32)],
            residual,
            part,
            left,
            right,
            edge_traces,
            from_rim,
            weights_h,
            weights_l,
            back,
            gather,
            rim_mask,
            scale,
            quotients,
        )
        sums = lax.all_to_all(
            sums.reshape(count, 1, POINTS), "dom", split_axis=0, concat_axis=0, tiled=True
        ).reshape(count, POINTS)
        (temperature,) = call(
            final_kernel,
            [((OWN, ELEMS, POINTS), F32)],
            sums,
            size,
            spectral_fields,
            residual,
            bend,
        )
    return momentum, temperature


def solution(mesh):
    placed = (
        P(None, "plane", "dom", None),
        P(),
        P(None, "dom", None),
        P(),
        P("dom"),
        P(),
        P("dom", None),
        P("dom", None, None),
        P(None, ("dom", "plane")),
    )
    return jax.shard_map(
        per_device,
        mesh=mesh,
        in_specs=placed,
        out_specs=(P(None, "plane", "dom", None), P("plane", "dom", None)),
        check_vma=False,
    )
```

```python
import functools

import jax
import jax.numpy as jnp
import numpy as np
from jax import lax
from jax.experimental import pallas as pl
from jax.experimental.pallas import tpu as pltpu
from jax.sharding import PartitionSpec as P

PLANES = 256
POINTS = 128
ELEMS = 64
OWN = 4
EDGES = 4
TRACE = 16
RIM = 32
ROWS = OWN * ELEMS
AXIAL_WAVE = 0.01
INVERSE_STEP = 0.5
LATENT = 2.0
F32 = jnp.float32
BF16 = jnp.bfloat16


def halves_np(table):
    high = table.astype(np.float32).astype(jnp.bfloat16)
    low = (table - high.astype(np.float64)).astype(np.float32).astype(jnp.bfloat16)
    return high, low


@functools.cache
def axial_table():
    points = np.arange(PLANES)[:, None]
    modes = np.arange(PLANES // 2)[None, :]
    angles = 2.0 * np.pi / PLANES * ((points * modes) % PLANES)
    others = np.where(modes == 0, 1.0 - 2.0 * (points % 2), np.sin(angles))
    return np.concatenate(halves_np(np.concatenate([np.cos(angles), others], axis=1)), axis=0)


def halves(value):
    high = value.astype(BF16)
    return high, (value - high.astype(F32)).astype(BF16)


def product(left, right):
    return jnp.dot(left, right, preferred_element_type=F32)


def across(left, right):
    return lax.dot_general(left, right, (((0,), (0,)), ((), ())), preferred_element_type=F32)


def product3(left, right):
    return product(left[0], right[0]) + (product(left[1], right[0]) + product(left[0], right[1]))


def lanes(rows):
    return lax.broadcasted_iota(jnp.int32, (rows, POINTS), 1)


def edge_of(lane):
    return (lane % (EDGES * TRACE)) // TRACE


def call(kernel, outs, *args, flops=0):
    return pl.pallas_call(
        kernel,
        out_shape=[jax.ShapeDtypeStruct(shape, kind) for shape, kind in outs],
        in_specs=[pl.BlockSpec(memory_space=pltpu.VMEM)] * len(args),
        out_specs=[pl.BlockSpec(memory_space=pltpu.VMEM)] * len(outs),
        compiler_params=pltpu.CompilerParams(vmem_limit_bytes=24 * 1024 * 1024),
        cost_estimate=pl.CostEstimate(
            flops=flops or 10**7,
            bytes_accessed=sum(a.size * a.dtype.itemsize for a in args),
            transcendentals=0,
        ),
    )(*args)


def stacked(value):
    return jnp.concatenate(halves(value), axis=1)


def product_stacked(value, high, low):
    pair = stacked(value)
    twice = jnp.concatenate([high, high], axis=0)
    return product(pair, twice) + product(pair[:, : low.shape[0]], low)


SLICES = 4


def pack_kernel(fields, out, taken, packed, arrivals, departures):
    width = ELEMS // SLICES
    into, back = [], []
    for part in range(SLICES):
        elements = pl.ds(part * width, width)
        rows = pl.ds(part * width * 16, width * 16)
        into.append(
            pltpu.make_async_copy(fields.at[:, :, elements, :], taken.at[:, :, elements, :], arrivals.at[part])
        )
        back.append(pltpu.make_async_copy(packed.at[rows, :], out.at[rows, :], departures.at[part]))
    for copy in into:
        copy.start()
    for part in range(SLICES):
        into[part].wait()
        for plane in range(OWN):
            for field in range(4):
                start = part * width * 16 + plane * 4 + field
                packed[pl.ds(start, width, stride=16), :] = taken[
                    field, plane, part * width : (part + 1) * width, :
                ]
        back[part].start()
    for copy in back:
        copy.wait()


def pack(fields):
    return pl.pallas_call(
        pack_kernel,
        out_shape=jax.ShapeDtypeStruct((ELEMS * 16, POINTS), F32),
        in_specs=[pl.BlockSpec(memory_space=pltpu.HBM)],
        out_specs=pl.BlockSpec(memory_space=pltpu.HBM),
        scratch_shapes=[
            pltpu.VMEM((4, OWN, ELEMS, POINTS), F32),
            pltpu.VMEM((ELEMS * 16, POINTS), F32),
            pltpu.SemaphoreType.DMA((SLICES,)),
            pltpu.SemaphoreType.DMA((SLICES,)),
        ],
        compiler_params=pltpu.CompilerParams(vmem_limit_bytes=60 * 1024 * 1024),
        cost_estimate=pl.CostEstimate(flops=10**6, bytes_accessed=2**20, transcendentals=0),
    )(fields)


def physical_kernel(fields, factors, melting, deriv_h, deriv_l, table, out):
    half = PLANES // 2
    even = [fields[pl.ds(c, half, stride=8), :] for c in range(4)]
    odd = [fields[pl.ds(4 + c, half, stride=8), :] for c in range(4)]
    even, odd = jnp.concatenate(even, axis=1), jnp.concatenate(odd, axis=1)
    mode = lax.broadcasted_iota(jnp.int32, (half, 4 * POINTS), 0)
    wave = mode.astype(F32) * AXIAL_WAVE
    spectral = jnp.concatenate(
        [jnp.concatenate([even, wave * odd], axis=1), jnp.concatenate([odd, -wave * even], axis=1)], axis=0
    )
    basis = (table[:PLANES], table[PLANES:])
    points = product3(basis, halves(spectral))
    values = [points[:, c * POINTS : (c + 1) * POINTS] for c in range(4)]
    axial = [points[:, c * POINTS : (c + 1) * POINTS] for c in range(4, 8)]
    first = values[0] * factors[0:1, :]
    second = values[1] * factors[1:2, :]
    third = values[2] * (-2.0 / PLANES)
    terms = []
    for c in range(4):
        slopes = product_stacked(values[c], deriv_h[...], deriv_l[...])
        term = first * slopes[:, :POINTS] + second * slopes[:, POINTS:] + third * axial[c]
        terms.append(term * melting[...] if c == 3 else term)
    terms = halves(jnp.concatenate(terms, axis=1))
    modal = across(basis[0], terms[0]) + (across(basis[1], terms[0]) + across(basis[0], terms[1]))
    row = lax.broadcasted_iota(jnp.int32, (PLANES, 4 * POINTS), 0)
    modal = jnp.where(row % half == 0, 0.5 * modal, modal)
    for c in range(4):
        out[pl.ds(c, half, stride=8), :] = modal[:half, c * POINTS : (c + 1) * POINTS]
        out[pl.ds(4 + c, half, stride=8), :] = modal[half:, c * POINTS : (c + 1) * POINTS]


def upright(row):
    size = row.shape[1]
    down = lax.broadcasted_iota(jnp.int32, (size, size), 0)
    along = lax.broadcasted_iota(jnp.int32, (size, size), 1)
    return jnp.sum(jnp.where(down == along, row, 0.0), axis=1, keepdims=True)


def exact(left, right):
    return jnp.dot(left, right, preferred_element_type=F32, precision=lax.Precision.HIGHEST)


def two_halves(doubled):
    high = doubled.astype(BF16).astype(F32)
    return jnp.where(lanes(doubled.shape[0]) < EDGES * TRACE, high, doubled - high)


def facing_local(split_traces, gather):
    edge = edge_of(lanes(ELEMS))
    parts = []
    for plane in range(OWN):
        own = split_traces[plane * ELEMS : (plane + 1) * ELEMS]
        stack = [jnp.where(edge == j, own, 0.0).astype(BF16) for j in range(EDGES)]
        parts.append(product(gather, jnp.concatenate(stack, axis=0)))
    return jnp.concatenate(parts, axis=0)


def packed_rims(rims, edge):
    lane = lanes(RIM)
    total = jnp.zeros((RIM, POINTS), F32)
    for plane in range(OWN):
        rows = rims[plane * RIM : (plane + 1) * RIM]
        for which in range(2):
            at = plane * 2 * TRACE + which * TRACE
            moved = pltpu.roll(rows, (at - which * EDGES * TRACE - edge * TRACE) % POINTS, 1)
            total = jnp.where((lane >= at) & (lane < at + TRACE), moved, total)
    return total


def unpacked_rims(packed, edge):
    lane = lanes(RIM)
    parts = []
    for plane in range(OWN):
        total = jnp.zeros((RIM, POINTS), F32)
        for which in range(2):
            at = which * EDGES * TRACE + edge * TRACE
            moved = pltpu.roll(packed, (at - plane * 2 * TRACE - which * TRACE) % POINTS, 1)
            total = jnp.where((lane >= at) & (lane < at + TRACE), moved, total)
        parts.append(total)
    return jnp.concatenate(parts, axis=0)


def doubled_sum(value):
    return value + pltpu.roll(value, EDGES * TRACE, 1)


def by_plane(rows):
    return jnp.concatenate(
        [jnp.broadcast_to(rows[plane : plane + 1], (ELEMS, POINTS)) for plane in range(OWN)], axis=0
    )


def squared_waves(number):
    plane = lax.axis_index("plane") * OWN + number
    wave = jnp.where(plane == 1, PLANES // 2, plane // 2).astype(F32) * AXIAL_WAVE
    return wave * wave


def by_element(rows):
    return jnp.concatenate([rows] * OWN, axis=0)


def start_helmholtz(vector, weights_h, weights_l, back, gather, to_rim, scale):
    scale = by_element(scale)
    images = product_stacked(vector, weights_h, weights_l)
    stiff, own, doubled, crossing, stiff_trace, own_trace = (
        images[:, k * POINTS : (k + 1) * POINTS] for k in range(6)
    )
    traces_split = two_halves(doubled)
    facing = facing_local(traces_split, gather).astype(BF16)
    coupling = product(jnp.concatenate([facing, facing], axis=1), back)
    part = scale * stiff + own - coupling[:, :POINTS]
    part_trace = scale * stiff_trace + own_trace - coupling[:, POINTS:]
    split = jnp.concatenate([traces_split, two_halves(part_trace)], axis=1).astype(BF16)
    rims = product(to_rim, split)
    first, second = doubled_sum(rims[:, :POINTS]), doubled_sum(rims[:, POINTS:])
    rims = jnp.where(lanes(ROWS) < EDGES * TRACE, first, second)
    half = OWN * RIM
    return part, packed_rims(rims[:half], 1), packed_rims(rims[half:], 3), doubled, crossing


def arrived(left, right, from_rim):
    both = jnp.concatenate([unpacked_rims(left[...], 3), unpacked_rims(right[...], 1)], axis=0)
    spread = product(from_rim[...], stacked(both))
    return spread[:, :POINTS], spread[:, POINTS:]


def rim_coupling(high, low, back):
    facing = jnp.where(
        lanes(ROWS) < EDGES * TRACE, high, pltpu.roll(low, EDGES * TRACE, 1)
    ).astype(BF16)
    return product(jnp.concatenate([facing, facing], axis=1), back[:, :POINTS])


def prepare_kernel(
    stiffness, traces, scale_row, near_rows, rim_rows, flags, deriv, geom, fields,
    weights_h, weights_l, back, gather, to_rim, from_rim, rim_mask, scale,
    size, melting, factors, deriv_h, deriv_l, part_out, left_out, right_out,
):
    plane_rank = lax.axis_index("plane")
    dom_rank = lax.axis_index("dom")
    edges = traces[...].reshape(EDGES * TRACE, POINTS)
    stiff = stiffness[...]
    sums = jnp.sum(jnp.abs(stiff), axis=0, keepdims=True)
    bound = 3.0 * jnp.max(sums, axis=1, keepdims=True) + 2.0 * jnp.sum(
        jnp.sum(edges * edges, axis=0, keepdims=True), axis=1, keepdims=True
    )
    bound = jnp.broadcast_to(bound, (1, POINTS))
    root = jnp.ones((1, POINTS), F32)
    for power in (32, 16, 8, 4, 2, 1):
        large = bound >= 4.0**power
        bound = jnp.where(large, bound * 4.0**-power, bound)
        root = jnp.where(large, root * 2.0**power, root)
    root = jnp.where(bound > 1.0, root * 2.0, root)
    size[...] = root * root
    inverse = 1.0 / root
    edges = edges * inverse
    stiff = stiff * inverse * inverse
    turned = jnp.concatenate([edges[2 * TRACE :], edges[: 2 * TRACE]], axis=0)
    edges = jnp.concatenate([edges, edges], axis=0)
    turned = jnp.concatenate([turned, turned], axis=0)
    edges_up = jnp.transpose(edges)
    turned_up = jnp.transpose(turned)
    own = 0.5 * exact(edges_up, edges)
    down = lax.broadcasted_iota(jnp.int32, (POINTS, POINTS), 0)
    along = lanes(POINTS)
    lower = EDGES * TRACE
    kept = (
        (down < lower)
        & (along >= lower)
        & (edge_of(down) == edge_of(along))
        & (edge_of(along) % 2 == 1)
    )
    crossing = exact(edges_up, jnp.where(kept, exact(turned, turned_up), 0.0))
    weights = jnp.concatenate(
        [stiff, own, turned_up, crossing, exact(stiff, turned_up), exact(own, turned_up)], axis=1
    )
    high, low = halves(weights)
    weights_h[...] = high
    weights_l[...] = low
    high, low = halves(jnp.concatenate([edges, exact(edges, turned_up)], axis=1))
    back[...] = jnp.concatenate([high, low], axis=0)

    rows = near_rows[...]
    rows = jnp.where(rows >= 0, rows - dom_rank * ELEMS, rows).astype(F32)
    near = [upright(rows[edge : edge + 1]).astype(jnp.int32) for edge in range(EDGES)]
    cell = lax.broadcasted_iota(jnp.int32, (ELEMS, EDGES * ELEMS), 1)
    wanted = near[EDGES - 1]
    for edge in range(EDGES - 1):
        wanted = jnp.where(cell // ELEMS == edge, near[edge], wanted)
    gather[...] = jnp.where(cell % ELEMS == wanted, 1.0, 0.0).astype(BF16)
    wide = lax.broadcasted_iota(jnp.int32, (ROWS, ROWS), 1)
    rims = [upright(rim_rows[side : side + 1, :].astype(F32)).astype(jnp.int32) for side in range(2)]
    column = jnp.concatenate([rims[side] + plane * ELEMS for side in range(2) for plane in range(OWN)], axis=0)
    picked = jnp.where(wide == column, 1.0, 0.0)
    to_rim[...] = picked.astype(BF16)
    from_rim[...] = jnp.transpose(picked).astype(BF16)
    lane = lanes(ELEMS)
    edge = edge_of(lane)
    beyond = ((edge == 1) & (near[1] == -2)) | ((edge == 3) & (near[3] == -2))
    mask = jnp.where(beyond & (lane >= lower), 1.0, 0.0)
    rim_mask[...] = mask
    scale[...] = jnp.broadcast_to(upright(scale_row[...]), (ELEMS, POINTS))

    melted = upright(flags[...].astype(F32))
    melting[...] = jnp.broadcast_to(1.0 / (1.0 + LATENT * melted), (PLANES, POINTS))
    for side in range(2):
        factors[side : side + 1, :] = geom[side, pl.ds(plane_rank, 1), :] * (-2.0 / PLANES)
    high, low = halves(jnp.concatenate([jnp.transpose(deriv[0]), jnp.transpose(deriv[1])], axis=1))
    deriv_h[...] = high
    deriv_l[...] = low

    vector = fields[3].reshape(ROWS, POINTS)
    part, left, right, _, _ = start_helmholtz(
        vector, weights_h[...], weights_l[...], back[...], gather[...], to_rim[...], scale[...]
    )
    part_out[...] = part
    left_out[...] = left
    right_out[...] = right


def base_kernel(fields, part, left, right, from_rim, back, size, table, out, table_out):
    table_out[...] = table[...]
    high, low = arrived(left, right, from_rim)
    image = part[...] - rim_coupling(high, low, back[...])
    squares = by_plane(squared_waves(lax.broadcasted_iota(jnp.int32, (OWN, POINTS), 0)))
    out[...] = -(squares * fields[3].reshape(ROWS, POINTS) + size[...] * image)


def residual_kernel(
    modal, base, weights_h, weights_l, back, gather, to_rim, scale,
    residual_out, part_out, left_out, right_out, traces_out,
):
    heat = [modal[pl.ds(plane * 4 + 3, ELEMS, stride=16), :] for plane in range(OWN)]
    residual = base[...] + jnp.concatenate(heat, axis=0)
    part, left, right, doubled, crossing = start_helmholtz(
        residual,
        weights_h[...],
        weights_l[...],
        back[...],
        gather[...],
        to_rim[...],
        scale[...],
    )
    left_out[...] = left
    right_out[...] = right
    residual_out[...] = residual
    part_out[...] = part
    lower = lanes(ROWS) < EDGES * TRACE
    traces_out[...] = jnp.where(lower, doubled, crossing)


def momentum_kernel(modal, residual, part, out, quotients):
    for field in range(3):
        for plane in range(OWN):
            out[field, plane] = modal[pl.ds(plane * 4 + field, ELEMS, stride=16), :]
    for plane in range(OWN):
        rows = pl.ds(plane * ELEMS, ELEMS)
        own = residual[rows, :]
        above = jnp.sum(jnp.sum(own * part[rows, :], axis=0, keepdims=True), axis=1, keepdims=True)
        below = jnp.sum(jnp.sum(own * own, axis=0, keepdims=True), axis=1, keepdims=True)
        quotient = jnp.where(below > 0.0, above / below, 0.0)
        quotients[plane : plane + 1, :] = jnp.broadcast_to(quotient, (1, POINTS))


NUMBERS = 9


def moments_kernel(
    residual_ref, part, left, right, traces_ref, from_rim, weights_h, weights_l, back, gather,
    rim_mask, scale, quotients, bend_out, sums_out,
):
    high, low = arrived(left, right, from_rim)
    beyond = high + low
    residual = residual_ref[...]
    bend = part[...] - rim_coupling(high, low, back[...]) - by_plane(quotients[...]) * residual
    bend_out[...] = bend
    weights = [
        jnp.concatenate([w[:, :POINTS], w[:, 2 * POINTS : 3 * POINTS]], axis=1)
        for w in (weights_h, weights_l)
    ]
    images = product_stacked(bend, *weights)
    stiff, doubled = images[:, :POINTS], images[:, POINTS:]
    traces = traces_ref[...]
    facing = doubled_sum(facing_local(two_halves(doubled), gather[...]))
    facing = facing + beyond - traces * by_element(rim_mask[...])
    own = pltpu.roll(doubled, 2 * TRACE, 1)
    upper = lanes(ROWS) >= EDGES * TRACE
    cubic = by_element(scale[...]) * (bend * stiff) + jnp.where(upper, own * (own - facing), 0.0)
    turned = jnp.where(
        edge_of(lanes(ROWS)) == 3,
        pltpu.roll(traces, 2 * TRACE, 1),
        pltpu.roll(traces, POINTS - 2 * TRACE, 1),
    )
    across_rims = jnp.where(upper, own * pltpu.roll(beyond, EDGES * TRACE, 1), turned * beyond)
    rows = [
        jnp.sum(value[plane * ELEMS : (plane + 1) * ELEMS], axis=0, keepdims=True)
        for value in (residual * residual, residual * bend, bend * bend, cubic, across_rims)
        for plane in range(OWN)
    ]
    whole, cut = jnp.concatenate(rows[: 4 * OWN], axis=0), jnp.concatenate(rows[4 * OWN :], axis=0)
    lane = lanes(OWN)
    cuts = [
        jnp.where((edge_of(lane) == edge) & ((lane >= EDGES * TRACE) == above), cut, 0.0)
        for above in (True, False)
        for edge in (3, 1)
    ]
    totals = jnp.sum(jnp.concatenate([whole, *cuts], axis=0), axis=1, keepdims=True)
    totals = jnp.concatenate([totals, quotients[:, 0:1], jnp.zeros((OWN, 1), F32)], axis=0)
    down = lax.broadcasted_iota(jnp.int32, ((NUMBERS + 1) * OWN, POINTS), 0)
    row = jnp.sum(jnp.where(down == lanes((NUMBERS + 1) * OWN), totals, 0.0), axis=0, keepdims=True)
    sums_out[...] = jnp.broadcast_to(row, sums_out.shape)


def final_kernel(sums, size, fields, residual, bend, out):
    diagonal = INVERSE_STEP + squared_waves(lanes(1))
    size = size[...]
    numbers = [pltpu.roll(sums[...], (-k * OWN) % POINTS, 1) for k in range(NUMBERS)]
    square, slant, bends, cubic, bend_left, bend_right, own_left, own_right, quotient = numbers

    def total(value):
        return jnp.sum(value, axis=0, keepdims=True)

    def beside(value):
        return pltpu.roll(value, 1, 0), pltpu.roll(value, value.shape[0] - 1, 0)

    k0 = total(square)
    k1 = total(quotient * square + slant)
    theta = k1 / k0
    apart = theta - quotient
    left, right = (apart - value for value in beside(apart))
    quotient_left, quotient_right = beside(quotient)
    norm = total(bends + apart * (apart * square - 2.0 * slant))
    bent = total(
        cubic
        + quotient_left * bend_left
        + quotient_right * bend_right
        - 2.0 * (apart * (bends + quotient * slant) + left * bend_left + right * bend_right)
        + apart * (apart * (slant + quotient * square) + left * own_left + right * own_right)
    )
    step = k0 / (diagonal * k0 + size * k1)
    length = step * size
    share = length * (norm / k0)
    ratio = length * share
    second = norm / (diagonal * norm + size * (bent - share * norm))
    second = jnp.where(norm > 0.0, second, 0.0)
    here = lax.broadcasted_iota(jnp.int32, apart.shape, 0) == lax.axis_index("dom")
    on_residual = step + second * (length * total(jnp.where(here, apart, 0.0)) + ratio)
    on_bend = -second * length
    for plane in range(OWN):
        rows = pl.ds(plane * ELEMS, ELEMS)
        out[plane] = (
            fields[3, plane]
            + on_residual[:, plane : plane + 1] * residual[rows, :]
            + on_bend[:, plane : plane + 1] * bend[rows, :]
        )


def per_device(
    spectral_fields,
    deriv_ops,
    geom,
    stiffness,
    stiff_scale,
    traces,
    neighbors,
    rim_lists,
    melt_flags,
):
    count = lax.axis_size("dom")
    groups = lax.axis_size("plane")
    whole = ((ROWS, POINTS), F32)
    rims = ((RIM, POINTS), F32)

    with jax.named_scope("to_points"):
        packed = pack(spectral_fields)
        gathered = lax.all_to_all(
            packed.reshape(groups, 16, POINTS), "plane", split_axis=0, concat_axis=0, tiled=True
        ).reshape(groups * 16, POINTS)

    def exchange(left, right):
        from_left = lax.ppermute(right, "dom", [(i, (i + 1) % count) for i in range(count)])
        from_right = lax.ppermute(left, "dom", [((i + 1) % count, i) for i in range(count)])
        return from_left, from_right

    with jax.named_scope("base"):
        (
            weights_h, weights_l, back, gather, to_rim, from_rim, rim_mask, scale,
            size, melting, factors, deriv_h, deriv_l, part, left, right,
        ) = call(
            prepare_kernel,
            [
                ((POINTS, 6 * POINTS), BF16),
                ((POINTS, 6 * POINTS), BF16),
                ((2 * POINTS, 2 * POINTS), BF16),
                ((ELEMS, EDGES * ELEMS), BF16),
                ((ROWS, ROWS), BF16),
                ((ROWS, ROWS), BF16),
                ((ELEMS, POINTS), F32),
                ((ELEMS, POINTS), F32),
                ((1, POINTS), F32),
                whole,
                ((2, POINTS), F32),
                ((POINTS, 2 * POINTS), BF16),
                ((POINTS, 2 * POINTS), BF16),
                whole,
                rims,
                rims,
            ],
            stiffness,
            traces,
            stiff_scale.reshape(1, ELEMS),
            neighbors.T,
            rim_lists[0],
            melt_flags.reshape(1, PLANES),
            deriv_ops,
            geom,
            spectral_fields,
        )
        left, right = exchange(left, right)
        table = jnp.asarray(axial_table())
        base, table = call(
            base_kernel,
            [whole, (table.shape, BF16)],
            spectral_fields,
            part,
            left,
            right,
            from_rim,
            back,
            size,
            table,
        )

    with jax.named_scope("advection"):
        gathered, base, table = lax.optimization_barrier((gathered, base, table))
        (modal,) = call(
            physical_kernel,
            [((groups * 16, POINTS), F32)],
            gathered,
            factors,
            melting,
            deriv_h,
            deriv_l,
            table,
            flops=10**9,
        )
        returned = lax.all_to_all(
            modal.reshape(groups, 16, POINTS), "plane", split_axis=0, concat_axis=0, tiled=True
        ).reshape(ELEMS * 16, POINTS)

    with jax.named_scope("solve"):
        residual, part, left, right, edge_traces = call(
            residual_kernel,
            [whole, whole, rims, rims, whole],
            returned,
            base,
            weights_h,
            weights_l,
            back,
            gather,
            to_rim,
            scale,
        )
        left, right = exchange(left, right)
        momentum, quotients = call(
            momentum_kernel,
            [((3, OWN, ELEMS, POINTS), F32), ((OWN, POINTS), F32)],
            returned,
            residual,
            part,
        )
        left, right, momentum = lax.optimization_barrier((left, right, momentum))
        bend, sums = call(
            moments_kernel,
            [whole, ((count, POINTS), F32)],
            residual,
            part,
            left,
            right,
            edge_traces,
            from_rim,
            weights_h,
            weights_l,
            back,
            gather,
            rim_mask,
            scale,
            quotients,
        )
        sums = lax.all_to_all(
            sums.reshape(count, 1, POINTS), "dom", split_axis=0, concat_axis=0, tiled=True
        ).reshape(count, POINTS)
        (temperature,) = call(
            final_kernel,
            [((OWN, ELEMS, POINTS), F32)],
            sums,
            size,
            spectral_fields,
            residual,
            bend,
        )
    return momentum, temperature


def solution(mesh):
    placed = (
        P(None, "plane", "dom", None),
        P(),
        P(None, "dom", None),
        P(),
        P("dom"),
        P(),
        P("dom", None),
        P("dom", None, None),
        P(None, ("dom", "plane")),
    )
    return jax.shard_map(
        per_device,
        mesh=mesh,
        in_specs=placed,
        out_specs=(P(None, "plane", "dom", None), P("plane", "dom", None)),
        check_vma=False,
    )
```

```python
import functools

import jax
import jax.numpy as jnp
import numpy as np
from jax import lax
from jax.experimental import pallas as pl
from jax.experimental.pallas import tpu as pltpu
from jax.sharding import PartitionSpec as P

PLANES = 256
POINTS = 128
ELEMS = 64
OWN = 4
EDGES = 4
TRACE = 16
RIM = 32
ROWS = OWN * ELEMS
AXIAL_WAVE = 0.01
INVERSE_STEP = 0.5
LATENT = 2.0
F32 = jnp.float32
BF16 = jnp.bfloat16


def halves_np(table):
    high = table.astype(np.float32).astype(jnp.bfloat16)
    low = (table - high.astype(np.float64)).astype(np.float32).astype(jnp.bfloat16)
    return high, low


@functools.cache
def axial_table():
    points = np.arange(PLANES)[:, None]
    modes = np.arange(PLANES // 2)[None, :]
    angles = 2.0 * np.pi / PLANES * ((points * modes) % PLANES)
    others = np.where(modes == 0, 1.0 - 2.0 * (points % 2), np.sin(angles))
    return np.concatenate(halves_np(np.concatenate([np.cos(angles), others], axis=1)), axis=0)


def halves(value):
    high = value.astype(BF16)
    return high, (value - high.astype(F32)).astype(BF16)


def product(left, right):
    return jnp.dot(left, right, preferred_element_type=F32)


def across(left, right):
    return lax.dot_general(left, right, (((0,), (0,)), ((), ())), preferred_element_type=F32)


def product3(left, right):
    return product(left[0], right[0]) + (product(left[1], right[0]) + product(left[0], right[1]))


def lanes(rows):
    return lax.broadcasted_iota(jnp.int32, (rows, POINTS), 1)


def edge_of(lane):
    return (lane % (EDGES * TRACE)) // TRACE


def call(kernel, outs, *args, flops=0):
    return pl.pallas_call(
        kernel,
        out_shape=[jax.ShapeDtypeStruct(shape, kind) for shape, kind in outs],
        in_specs=[pl.BlockSpec(memory_space=pltpu.VMEM)] * len(args),
        out_specs=[pl.BlockSpec(memory_space=pltpu.VMEM)] * len(outs),
        compiler_params=pltpu.CompilerParams(vmem_limit_bytes=24 * 1024 * 1024),
        cost_estimate=pl.CostEstimate(
            flops=flops or 10**7,
            bytes_accessed=sum(a.size * a.dtype.itemsize for a in args),
            transcendentals=0,
        ),
    )(*args)


def stacked(value):
    return jnp.concatenate(halves(value), axis=1)


def product_stacked(value, high, low):
    pair = stacked(value)
    twice = jnp.concatenate([high, high], axis=0)
    return product(pair, twice) + product(pair[:, : low.shape[0]], low)


SLICES = 4


def pack_kernel(fields, out, taken, packed, arrivals, departures):
    width = ELEMS // SLICES
    into, back = [], []
    for part in range(SLICES):
        elements = pl.ds(part * width, width)
        rows = pl.ds(part * width * 16, width * 16)
        into.append(
            pltpu.make_async_copy(fields.at[:, :, elements, :], taken.at[:, :, elements, :], arrivals.at[part])
        )
        back.append(pltpu.make_async_copy(packed.at[rows, :], out.at[rows, :], departures.at[part]))
    for copy in into:
        copy.start()
    for part in range(SLICES):
        into[part].wait()
        for plane in range(OWN):
            for field in range(4):
                start = part * width * 16 + plane * 4 + field
                packed[pl.ds(start, width, stride=16), :] = taken[
                    field, plane, part * width : (part + 1) * width, :
                ]
        back[part].start()
    for copy in back:
        copy.wait()


def pack(fields):
    return pl.pallas_call(
        pack_kernel,
        out_shape=jax.ShapeDtypeStruct((ELEMS * 16, POINTS), F32),
        in_specs=[pl.BlockSpec(memory_space=pltpu.HBM)],
        out_specs=pl.BlockSpec(memory_space=pltpu.HBM),
        scratch_shapes=[
            pltpu.VMEM((4, OWN, ELEMS, POINTS), F32),
            pltpu.VMEM((ELEMS * 16, POINTS), F32),
            pltpu.SemaphoreType.DMA((SLICES,)),
            pltpu.SemaphoreType.DMA((SLICES,)),
        ],
        compiler_params=pltpu.CompilerParams(vmem_limit_bytes=60 * 1024 * 1024),
        cost_estimate=pl.CostEstimate(flops=10**6, bytes_accessed=2**20, transcendentals=0),
    )(fields)


def physical_kernel(fields, factors, melting, deriv_h, deriv_l, table, out):
    half = PLANES // 2
    even = [fields[pl.ds(c, half, stride=8), :] for c in range(4)]
    odd = [fields[pl.ds(4 + c, half, stride=8), :] for c in range(4)]
    even, odd = jnp.concatenate(even, axis=1), jnp.concatenate(odd, axis=1)
    mode = lax.broadcasted_iota(jnp.int32, (half, 4 * POINTS), 0)
    wave = mode.astype(F32) * AXIAL_WAVE
    spectral = jnp.concatenate(
        [jnp.concatenate([even, wave * odd], axis=1), jnp.concatenate([odd, -wave * even], axis=1)], axis=0
    )
    basis = (table[:PLANES], table[PLANES:])
    points = product3(basis, halves(spectral))
    values = [points[:, c * POINTS : (c + 1) * POINTS] for c in range(4)]
    axial = [points[:, c * POINTS : (c + 1) * POINTS] for c in range(4, 8)]
    first = values[0] * factors[0:1, :]
    second = values[1] * factors[1:2, :]
    third = values[2] * (-2.0 / PLANES)
    terms = []
    for c in range(4):
        slopes = product_stacked(values[c], deriv_h[...], deriv_l[...])
        term = first * slopes[:, :POINTS] + second * slopes[:, POINTS:] + third * axial[c]
        terms.append(term * melting[...] if c == 3 else term)
    terms = halves(jnp.concatenate(terms, axis=1))
    modal = across(basis[0], terms[0]) + (across(basis[1], terms[0]) + across(basis[0], terms[1]))
    row = lax.broadcasted_iota(jnp.int32, (PLANES, 4 * POINTS), 0)
    modal = jnp.where(row % half == 0, 0.5 * modal, modal)
    for c in range(4):
        out[pl.ds(c, half, stride=8), :] = modal[:half, c * POINTS : (c + 1) * POINTS]
        out[pl.ds(4 + c, half, stride=8), :] = modal[half:, c * POINTS : (c + 1) * POINTS]


def upright(row):
    size = row.shape[1]
    down = lax.broadcasted_iota(jnp.int32, (size, size), 0)
    along = lax.broadcasted_iota(jnp.int32, (size, size), 1)
    return jnp.sum(jnp.where(down == along, row, 0.0), axis=1, keepdims=True)


def exact(left, right):
    return jnp.dot(left, right, preferred_element_type=F32, precision=lax.Precision.HIGHEST)


def two_halves(doubled):
    high = doubled.astype(BF16).astype(F32)
    return jnp.where(lanes(doubled.shape[0]) < EDGES * TRACE, high, doubled - high)


def facing_local(split_traces, gather):
    edge = edge_of(lanes(ELEMS))
    parts = []
    for plane in range(OWN):
        own = split_traces[plane * ELEMS : (plane + 1) * ELEMS]
        stack = [jnp.where(edge == j, own, 0.0).astype(BF16) for j in range(EDGES)]
        parts.append(product(gather, jnp.concatenate(stack, axis=0)))
    return jnp.concatenate(parts, axis=0)


def packed_rims(rims, edge):
    lane = lanes(RIM)
    total = jnp.zeros((RIM, POINTS), F32)
    for plane in range(OWN):
        rows = rims[plane * RIM : (plane + 1) * RIM]
        for which in range(2):
            at = plane * 2 * TRACE + which * TRACE
            moved = pltpu.roll(rows, (at - which * EDGES * TRACE - edge * TRACE) % POINTS, 1)
            total = jnp.where((lane >= at) & (lane < at + TRACE), moved, total)
    return total


def unpacked_rims(packed, edge):
    lane = lanes(RIM)
    parts = []
    for plane in range(OWN):
        total = jnp.zeros((RIM, POINTS), F32)
        for which in range(2):
            at = which * EDGES * TRACE + edge * TRACE
            moved = pltpu.roll(packed, (at - plane * 2 * TRACE - which * TRACE) % POINTS, 1)
            total = jnp.where((lane >= at) & (lane < at + TRACE), moved, total)
        parts.append(total)
    return jnp.concatenate(parts, axis=0)


def doubled_sum(value):
    return value + pltpu.roll(value, EDGES * TRACE, 1)


def by_plane(rows):
    return jnp.concatenate(
        [jnp.broadcast_to(rows[plane : plane + 1], (ELEMS, POINTS)) for plane in range(OWN)], axis=0
    )


def squared_waves(number):
    plane = lax.axis_index("plane") * OWN + number
    wave = jnp.where(plane == 1, PLANES // 2, plane // 2).astype(F32) * AXIAL_WAVE
    return wave * wave


def by_element(rows):
    return jnp.concatenate([rows] * OWN, axis=0)


def start_helmholtz(vector, weights_h, weights_l, back, gather, to_rim, scale):
    scale = by_element(scale)
    images = product_stacked(vector, weights_h, weights_l)
    stiff, own, doubled, crossing, stiff_trace, own_trace = (
        images[:, k * POINTS : (k + 1) * POINTS] for k in range(6)
    )
    traces_split = two_halves(doubled)
    facing = facing_local(traces_split, gather).astype(BF16)
    coupling = product(jnp.concatenate([facing, facing], axis=1), back[:, : 2 * POINTS])
    part = scale * stiff + own - coupling[:, :POINTS]
    part_trace = scale * stiff_trace + own_trace - coupling[:, POINTS:]
    split = jnp.concatenate([traces_split, two_halves(part_trace)], axis=1).astype(BF16)
    rims = product(to_rim, split)
    first, second = doubled_sum(rims[:, :POINTS]), doubled_sum(rims[:, POINTS:])
    rims = jnp.where(lanes(ROWS) < EDGES * TRACE, first, second)
    half = OWN * RIM
    return part, packed_rims(rims[:half], 1), packed_rims(rims[half:], 3), doubled, crossing


def arrived(left, right, from_rim):
    both = jnp.concatenate([unpacked_rims(left[...], 3), unpacked_rims(right[...], 1)], axis=0)
    spread = product(from_rim[...], stacked(both))
    return spread[:, :POINTS], spread[:, POINTS:]


def rim_coupling(high, low, back):
    facing = jnp.where(
        lanes(ROWS) < EDGES * TRACE, high, pltpu.roll(low, EDGES * TRACE, 1)
    ).astype(BF16)
    return product(jnp.concatenate([facing, facing], axis=1), back)


def prepare_kernel(
    stiffness, traces, scale_row, near_rows, rim_rows, flags, deriv, geom, fields,
    weights_h, weights_l, back, gather, to_rim, from_rim, rim_mask, scale,
    size, melting, factors, deriv_h, deriv_l, part_out, left_out, right_out,
):
    plane_rank = lax.axis_index("plane")
    dom_rank = lax.axis_index("dom")
    edges = traces[...].reshape(EDGES * TRACE, POINTS)
    stiff = stiffness[...]
    sums = jnp.sum(jnp.abs(stiff), axis=0, keepdims=True)
    bound = 3.0 * jnp.max(sums, axis=1, keepdims=True) + 2.0 * jnp.sum(
        jnp.sum(edges * edges, axis=0, keepdims=True), axis=1, keepdims=True
    )
    bound = jnp.broadcast_to(bound, (1, POINTS))
    root = jnp.ones((1, POINTS), F32)
    for power in (32, 16, 8, 4, 2, 1):
        large = bound >= 4.0**power
        bound = jnp.where(large, bound * 4.0**-power, bound)
        root = jnp.where(large, root * 2.0**power, root)
    root = jnp.where(bound > 1.0, root * 2.0, root)
    size[...] = root * root
    inverse = 1.0 / root
    edges = edges * inverse
    stiff = stiff * inverse * inverse
    turned = jnp.concatenate([edges[2 * TRACE :], edges[: 2 * TRACE]], axis=0)
    edges = jnp.concatenate([edges, edges], axis=0)
    turned = jnp.concatenate([turned, turned], axis=0)
    edges_up = jnp.transpose(edges)
    turned_up = jnp.transpose(turned)
    own = 0.5 * exact(edges_up, edges)
    down = lax.broadcasted_iota(jnp.int32, (POINTS, POINTS), 0)
    along = lanes(POINTS)
    lower = EDGES * TRACE
    kept = (
        (down < lower)
        & (along >= lower)
        & (edge_of(down) == edge_of(along))
        & (edge_of(along) % 2 == 1)
    )
    crossing = exact(edges_up, jnp.where(kept, exact(turned, turned_up), 0.0))
    weights = jnp.concatenate(
        [stiff, own, turned_up, crossing, exact(stiff, turned_up), exact(own, turned_up)], axis=1
    )
    high, low = halves(weights)
    weights_h[...] = high
    weights_l[...] = low
    high, low = halves(jnp.concatenate([edges, exact(edges, turned_up), exact(edges, stiff)], axis=1))
    back[...] = jnp.concatenate([high, low], axis=0)

    rows = near_rows[...]
    rows = jnp.where(rows >= 0, rows - dom_rank * ELEMS, rows).astype(F32)
    near = [upright(rows[edge : edge + 1]).astype(jnp.int32) for edge in range(EDGES)]
    cell = lax.broadcasted_iota(jnp.int32, (ELEMS, EDGES * ELEMS), 1)
    wanted = near[EDGES - 1]
    for edge in range(EDGES - 1):
        wanted = jnp.where(cell // ELEMS == edge, near[edge], wanted)
    gather[...] = jnp.where(cell % ELEMS == wanted, 1.0, 0.0).astype(BF16)
    wide = lax.broadcasted_iota(jnp.int32, (ROWS, ROWS), 1)
    rims = [upright(rim_rows[side : side + 1, :].astype(F32)).astype(jnp.int32) for side in range(2)]
    column = jnp.concatenate([rims[side] + plane * ELEMS for side in range(2) for plane in range(OWN)], axis=0)
    picked = jnp.where(wide == column, 1.0, 0.0)
    to_rim[...] = picked.astype(BF16)
    from_rim[...] = jnp.transpose(picked).astype(BF16)
    lane = lanes(ELEMS)
    edge = edge_of(lane)
    beyond = ((edge == 1) & (near[1] == -2)) | ((edge == 3) & (near[3] == -2))
    mask = jnp.where(beyond & (lane >= lower), 1.0, 0.0)
    rim_mask[...] = mask
    scale[...] = jnp.broadcast_to(upright(scale_row[...]), (ELEMS, POINTS))

    melted = upright(flags[...].astype(F32))
    melting[...] = jnp.broadcast_to(1.0 / (1.0 + LATENT * melted), (PLANES, POINTS))
    for side in range(2):
        factors[side : side + 1, :] = geom[side, pl.ds(plane_rank, 1), :] * (-2.0 / PLANES)
    high, low = halves(jnp.concatenate([jnp.transpose(deriv[0]), jnp.transpose(deriv[1])], axis=1))
    deriv_h[...] = high
    deriv_l[...] = low

    vector = fields[3].reshape(ROWS, POINTS)
    part, left, right, _, _ = start_helmholtz(
        vector, weights_h[...], weights_l[...], back[...], gather[...], to_rim[...], scale[...]
    )
    part_out[...] = part
    left_out[...] = left
    right_out[...] = right


def base_kernel(fields, part, left, right, from_rim, back, size, table, out, table_out):
    table_out[...] = table[...]
    high, low = arrived(left, right, from_rim)
    image = part[...] - rim_coupling(high, low, back[:, :POINTS])
    squares = by_plane(squared_waves(lax.broadcasted_iota(jnp.int32, (OWN, POINTS), 0)))
    out[...] = -(squares * fields[3].reshape(ROWS, POINTS) + size[...] * image)


def residual_kernel(
    modal, base, weights_h, weights_l, back, gather, to_rim, scale,
    residual_out, part_out, left_out, right_out, traces_out,
):
    heat = [modal[pl.ds(plane * 4 + 3, ELEMS, stride=16), :] for plane in range(OWN)]
    residual = base[...] + jnp.concatenate(heat, axis=0)
    part, left, right, doubled, crossing = start_helmholtz(
        residual,
        weights_h[...],
        weights_l[...],
        back[...],
        gather[...],
        to_rim[...],
        scale[...],
    )
    left_out[...] = left
    right_out[...] = right
    residual_out[...] = residual
    part_out[...] = part
    lower = lanes(ROWS) < EDGES * TRACE
    traces_out[...] = jnp.where(lower, doubled, crossing)


def momentum_kernel(
    modal, residual_ref, part, weights_h, weights_l, gather, out, quotients, bend_out, stiff_out, doubled_out, facing_out
):
    residual = residual_ref[...]
    rows = []
    for plane in range(OWN):
        own = residual[plane * ELEMS : (plane + 1) * ELEMS]
        image = part[plane * ELEMS : (plane + 1) * ELEMS, :]
        above = jnp.sum(jnp.sum(own * image, axis=0, keepdims=True), axis=1, keepdims=True)
        below = jnp.sum(jnp.sum(own * own, axis=0, keepdims=True), axis=1, keepdims=True)
        rows.append(jnp.broadcast_to(jnp.where(below > 0.0, above / below, 0.0), (1, POINTS)))
    rows = jnp.concatenate(rows, axis=0)
    quotients[...] = rows
    bend = part[...] - by_plane(rows) * residual
    weights = [
        jnp.concatenate([w[:, :POINTS], w[:, 2 * POINTS : 3 * POINTS]], axis=1)
        for w in (weights_h, weights_l)
    ]
    images = product_stacked(bend, *weights)
    stiff, doubled = images[:, :POINTS], images[:, POINTS:]
    bend_out[...] = bend
    stiff_out[...] = stiff
    doubled_out[...] = doubled
    facing_out[...] = doubled_sum(facing_local(two_halves(doubled), gather[...]))
    for field in range(3):
        for plane in range(OWN):
            out[field, plane] = modal[pl.ds(plane * 4 + field, ELEMS, stride=16), :]


NUMBERS = 9


def moments_kernel(
    residual_ref, bend_ref, stiff_ref, doubled_ref, facing_ref, left, right, traces_ref, from_rim, back, gather,
    rim_mask, scale, quotients, bend_out, sums_out,
):
    high, low = arrived(left, right, from_rim)
    beyond = high + low
    residual = residual_ref[...]
    coupling = rim_coupling(high, low, back[...])
    bend = bend_ref[...] - coupling[:, :POINTS]
    bend_out[...] = bend
    stiff = stiff_ref[...] - coupling[:, 2 * POINTS :]
    more = coupling[:, POINTS : 2 * POINTS]
    doubled = doubled_ref[...] - more
    traces = traces_ref[...]
    facing = facing_ref[...] - doubled_sum(facing_local(two_halves(more), gather[...]))
    facing = facing + beyond - traces * by_element(rim_mask[...])
    own = pltpu.roll(doubled, 2 * TRACE, 1)
    upper = lanes(ROWS) >= EDGES * TRACE
    cubic = by_element(scale[...]) * (bend * stiff) + jnp.where(upper, own * (own - facing), 0.0)
    turned = jnp.where(
        edge_of(lanes(ROWS)) == 3,
        pltpu.roll(traces, 2 * TRACE, 1),
        pltpu.roll(traces, POINTS - 2 * TRACE, 1),
    )
    across_rims = jnp.where(upper, own * pltpu.roll(beyond, EDGES * TRACE, 1), turned * beyond)
    rows = [
        jnp.sum(value[plane * ELEMS : (plane + 1) * ELEMS], axis=0, keepdims=True)
        for value in (residual * residual, residual * bend, bend * bend, cubic, across_rims)
        for plane in range(OWN)
    ]
    whole, cut = jnp.concatenate(rows[: 4 * OWN], axis=0), jnp.concatenate(rows[4 * OWN :], axis=0)
    lane = lanes(OWN)
    cuts = [
        jnp.where((edge_of(lane) == edge) & ((lane >= EDGES * TRACE) == above), cut, 0.0)
        for above in (True, False)
        for edge in (3, 1)
    ]
    totals = jnp.sum(jnp.concatenate([whole, *cuts], axis=0), axis=1, keepdims=True)
    totals = jnp.concatenate([totals, quotients[:, 0:1], jnp.zeros((OWN, 1), F32)], axis=0)
    down = lax.broadcasted_iota(jnp.int32, ((NUMBERS + 1) * OWN, POINTS), 0)
    row = jnp.sum(jnp.where(down == lanes((NUMBERS + 1) * OWN), totals, 0.0), axis=0, keepdims=True)
    sums_out[...] = jnp.broadcast_to(row, sums_out.shape)


def final_kernel(sums, size, fields, residual, bend, out):
    diagonal = INVERSE_STEP + squared_waves(lanes(1))
    size = size[...]
    numbers = [pltpu.roll(sums[...], (-k * OWN) % POINTS, 1) for k in range(NUMBERS)]
    square, slant, bends, cubic, bend_left, bend_right, own_left, own_right, quotient = numbers

    def total(value):
        return jnp.sum(value, axis=0, keepdims=True)

    def beside(value):
        return pltpu.roll(value, 1, 0), pltpu.roll(value, value.shape[0] - 1, 0)

    k0 = total(square)
    k1 = total(quotient * square + slant)
    theta = k1 / k0
    apart = theta - quotient
    left, right = (apart - value for value in beside(apart))
    quotient_left, quotient_right = beside(quotient)
    norm = total(bends + apart * (apart * square - 2.0 * slant))
    bent = total(
        cubic
        + quotient_left * bend_left
        + quotient_right * bend_right
        - 2.0 * (apart * (bends + quotient * slant) + left * bend_left + right * bend_right)
        + apart * (apart * (slant + quotient * square) + left * own_left + right * own_right)
    )
    step = k0 / (diagonal * k0 + size * k1)
    length = step * size
    share = length * (norm / k0)
    ratio = length * share
    second = norm / (diagonal * norm + size * (bent - share * norm))
    second = jnp.where(norm > 0.0, second, 0.0)
    here = lax.broadcasted_iota(jnp.int32, apart.shape, 0) == lax.axis_index("dom")
    on_residual = step + second * (length * total(jnp.where(here, apart, 0.0)) + ratio)
    on_bend = -second * length
    for plane in range(OWN):
        rows = pl.ds(plane * ELEMS, ELEMS)
        out[plane] = (
            fields[3, plane]
            + on_residual[:, plane : plane + 1] * residual[rows, :]
            + on_bend[:, plane : plane + 1] * bend[rows, :]
        )


def per_device(
    spectral_fields,
    deriv_ops,
    geom,
    stiffness,
    stiff_scale,
    traces,
    neighbors,
    rim_lists,
    melt_flags,
):
    count = lax.axis_size("dom")
    groups = lax.axis_size("plane")
    whole = ((ROWS, POINTS), F32)
    rims = ((RIM, POINTS), F32)

    with jax.named_scope("to_points"):
        packed = pack(spectral_fields)
        gathered = lax.all_to_all(
            packed.reshape(groups, 16, POINTS), "plane", split_axis=0, concat_axis=0, tiled=True
        ).reshape(groups * 16, POINTS)

    def exchange(left, right):
        from_left = lax.ppermute(right, "dom", [(i, (i + 1) % count) for i in range(count)])
        from_right = lax.ppermute(left, "dom", [((i + 1) % count, i) for i in range(count)])
        return from_left, from_right

    with jax.named_scope("base"):
        (
            weights_h, weights_l, back, gather, to_rim, from_rim, rim_mask, scale,
            size, melting, factors, deriv_h, deriv_l, part, left, right,
        ) = call(
            prepare_kernel,
            [
                ((POINTS, 6 * POINTS), BF16),
                ((POINTS, 6 * POINTS), BF16),
                ((2 * POINTS, 3 * POINTS), BF16),
                ((ELEMS, EDGES * ELEMS), BF16),
                ((ROWS, ROWS), BF16),
                ((ROWS, ROWS), BF16),
                ((ELEMS, POINTS), F32),
                ((ELEMS, POINTS), F32),
                ((1, POINTS), F32),
                whole,
                ((2, POINTS), F32),
                ((POINTS, 2 * POINTS), BF16),
                ((POINTS, 2 * POINTS), BF16),
                whole,
                rims,
                rims,
            ],
            stiffness,
            traces,
            stiff_scale.reshape(1, ELEMS),
            neighbors.T,
            rim_lists[0],
            melt_flags.reshape(1, PLANES),
            deriv_ops,
            geom,
            spectral_fields,
        )
        left, right = exchange(left, right)
        table = jnp.asarray(axial_table())
        base, table = call(
            base_kernel,
            [whole, (table.shape, BF16)],
            spectral_fields,
            part,
            left,
            right,
            from_rim,
            back,
            size,
            table,
        )

    with jax.named_scope("advection"):
        gathered, base, table = lax.optimization_barrier((gathered, base, table))
        (modal,) = call(
            physical_kernel,
            [((groups * 16, POINTS), F32)],
            gathered,
            factors,
            melting,
            deriv_h,
            deriv_l,
            table,
            flops=10**9,
        )
        returned = lax.all_to_all(
            modal.reshape(groups, 16, POINTS), "plane", split_axis=0, concat_axis=0, tiled=True
        ).reshape(ELEMS * 16, POINTS)

    with jax.named_scope("solve"):
        residual, part, left, right, edge_traces = call(
            residual_kernel,
            [whole, whole, rims, rims, whole],
            returned,
            base,
            weights_h,
            weights_l,
            back,
            gather,
            to_rim,
            scale,
        )
        left, right = exchange(left, right)
        momentum, quotients, bend, stiff, doubled, facing = call(
            momentum_kernel,
            [((3, OWN, ELEMS, POINTS), F32), ((OWN, POINTS), F32), whole, whole, whole, whole],
            returned,
            residual,
            part,
            weights_h,
            weights_l,
            gather,
        )
        left, right, momentum = lax.optimization_barrier((left, right, momentum))
        bend, sums = call(
            moments_kernel,
            [whole, ((count, POINTS), F32)],
            residual,
            bend,
            stiff,
            doubled,
            facing,
            left,
            right,
            edge_traces,
            from_rim,
            back,
            gather,
            rim_mask,
            scale,
            quotients,
        )
        sums = lax.all_to_all(
            sums.reshape(count, 1, POINTS), "dom", split_axis=0, concat_axis=0, tiled=True
        ).reshape(count, POINTS)
        (temperature,) = call(
            final_kernel,
            [((OWN, ELEMS, POINTS), F32)],
            sums,
            size,
            spectral_fields,
            residual,
            bend,
        )
    return momentum, temperature


def solution(mesh):
    placed = (
        P(None, "plane", "dom", None),
        P(),
        P(None, "dom", None),
        P(),
        P("dom"),
        P(),
        P("dom", None),
        P("dom", None, None),
        P(None, ("dom", "plane")),
    )
    return jax.shard_map(
        per_device,
        mesh=mesh,
        in_specs=placed,
        out_specs=(P(None, "plane", "dom", None), P("plane", "dom", None)),
        check_vma=False,
    )
```
